128 devices in a mesh: row: 16 (over x, y), col: 8 (over z, core).
Axes of the slice: x: 4, y: 4, z: 4, core: 2. Of those that a mesh axis runs over, the one named last changes fastest.
Arguments:
- coefficients: bfloat16 [10240, 32, 256], P('row'), may hold values from -0.59765625 to 0.59765625
- range_start: int32 [80], replicated, may hold values from 0 to 127
- range_end: int32 [80], replicated, may hold values from 129 to 256
- pair_list: int32 [1976, 2], replicated, may hold values from 0 to 79, as said below
Outputs:
- exchange_matrix: float32 [10240, 10, 8, 128], P('row', None, 'col')
The draws below stay inside these ranges and needn't reach their ends.
Inputs may be any that keep to these rules, and one draw needn't show every extreme that they name: `pair_list`: 1976 distinct unordered block pairs, the smaller block first; every block is listed with itself.
All inputs are finite; a program needn't handle non-finite values.
Results may differ from the reference program's by a relative error of at most 0.0003.
Values may be sent and summed in bfloat16 or wider, within the bound.
No kernel may reach another device: no remote copies, remote signals or barrier semaphores. Data moves between devices by JAX's collectives and lax.ppermute only.
A program may use at most 192 MiB of HBM per device.

```python
import jax
import jax.numpy as jnp
import numpy as np
from jax import lax

BLK = 128
NAUX = 32
OCC = 256
NBLK = 80
NB = 10240
NPAIR = 1976
N_COL = 8


def draw_pair_list(key, part):
    key = jax.random.fold_in(key, 11)
    upper_rows, upper_cols = np.triu_indices(NBLK)
    upper_count = upper_rows.shape[0]
    first_side = jnp.asarray(upper_rows, jnp.int32)
    second_side = jnp.asarray(upper_cols, jnp.int32)
    random_score = jax.random.randint(key, (upper_count,), 0, 4096, dtype=jnp.int32)
    distance = second_side - first_side
    priority = jnp.where(distance == 0, 20000, random_score - 16 * distance)
    ranked = priority * 16384 + jnp.arange(upper_count, dtype=jnp.int32)
    chosen = lax.top_k(ranked, NPAIR)[1]
    return jnp.stack([first_side[chosen], second_side[chosen]], axis=1)


def touch_ends(drawn, own_key, low, high):
    longest = drawn.shape.index(max(drawn.shape))
    spots = []
    for shift in (0, 1):
        where = [jax.random.randint(jax.random.fold_in(own_key, axis), (), 0, length) for axis, length in enumerate(drawn.shape)]
        where[longest] = (where[longest] + shift) % drawn.shape[longest]
        spots.append(tuple(where))
    return drawn.at[spots[0]].set(low).at[spots[1]].set(high)


def block_levels(key, dims, split, low, high):
    def one(position, parts):
        heights = jax.random.uniform(jax.random.fold_in(jax.random.fold_in(key, 6), position), (parts,), jnp.float32, low / len(split), high / len(split))
        return jnp.repeat(jnp.exp(heights), dims[position] // parts).reshape((-1,) + (1,) * (len(dims) - position - 1))

    gain = one(*split[0])
    for cut in split[1:]:
        gain = gain * one(*cut)
    return gain


def centred(stream_key, extent, spread, reach, cuts=(), kind=jnp.bfloat16):
    entries = spread * jax.random.normal(stream_key, extent, jnp.float32)
    if cuts:
        entries = entries * block_levels(stream_key, extent, cuts, -0.22, 0.18)
    return jnp.clip(entries, -reach, reach).astype(kind)


def setup_inputs(seed: int = 0) -> dict:
    key_of = jax.random.split(jax.random.key(seed), 5)
    coefficients = centred(key_of[0], (NB, NAUX, OCC), 0.1, 0.59765625, ((0, 16),))
    range_start = touch_ends(jax.random.randint(key_of[1], (NBLK,), 0, OCC // 2), jax.random.fold_in(key_of[1], 1), 0, (OCC // 2) - 1).astype(jnp.int32)
    range_end = touch_ends(jax.random.randint(key_of[2], (NBLK,), OCC // 2 + 1, OCC + 1), jax.random.fold_in(key_of[2], 1), OCC // 2 + 1, OCC).astype(jnp.int32)
    pair_list = draw_pair_list(jax.random.fold_in(key_of[4], 71), 0)
    return dict(coefficients=coefficients, range_start=range_start, range_end=range_end, pair_list=pair_list)


def listed_matrix(pair_list, block_count):
    marked = jnp.zeros((block_count, block_count), jnp.int32).at[pair_list[:, 0], pair_list[:, 1]].set(1)
    return jnp.maximum(marked, marked.T)


def reference(coefficients, range_start, range_end, pair_list):
    orbital = jnp.arange(OCC, dtype=jnp.int32)
    inside = (orbital[None, :] >= range_start[:, None]) & (orbital[None, :] < range_end[:, None])
    masked = coefficients.reshape(NBLK, BLK, NAUX, OCC) * inside[:, None, None, :].astype(jnp.bfloat16)
    masked = masked.reshape(NB, NAUX * OCC)
    product = jnp.dot(masked, masked.T, preferred_element_type=jnp.float32)
    listed = listed_matrix(pair_list, NBLK).astype(jnp.float32)
    product = product.reshape(NBLK, BLK, NBLK, BLK) * listed[:, None, :, None]
    return product.reshape(NB, NBLK // N_COL, N_COL, BLK)
```

```python
import functools

import jax
import jax.numpy as jnp
import numpy as np
from jax import lax
from jax.experimental import pallas as pl
from jax.experimental.pallas import tpu as pltpu
from jax.sharding import PartitionSpec as P

BLK = 128
NX, NY, NZ, NCORE = 4, 4, 4, 2
NCOL = NZ * NCORE
NDEV = NX * NY * NCOL
LOCAL = 5
ROWS = LOCAL * BLK
NAUX, OCC = 32, 256
NSL = 8
SLW = NAUX * OCC // NSL
AXES = ("row", "col")

PARENT = (None, 0, 0, 1, 0, 1, 2, 3)
EMBED = (
    (3, 7, 8, 4, 8, 4, 8, 4, 8, 4, 0, 11, 0, 7, 0, 3, 3, 11, 3, 11),
    (3, 0, 3, 0, 3, 0, 2, 1, 11, 8, 11, 4, 11, 4, 11, 4, 11, 4, 11, 4),
    (10, 1, 10, 1, 10, 4, 10, 1, 10, 1, 11, 6, 2, 6, 6, 1, 2, 6, 2, 6),
    (2, 1, 7, 8, 2, 1, 2, 1, 7, 8, 6, 5, 6, 5, 6, 5, 6, 5, 6, 0),
)
ORDER = ((0, 1), (1, 1), (0, 2), (0, 3), (1, 2), (1, 3), (0, 4), (0, 5), (0, 6), (0, 7), (1, 4), (1, 5), (1, 6), (1, 7))
GROUPS = ((0, 1), (2, 3), (4,))
REACH = (5, 6, 7)


def dev(x, y, z, core):
    return ((x * NY + y) * NZ + z) * NCORE + core


def embeddings():
    found = []

    def grow(at):
        if len(at) == 8:
            found.append(tuple(at))
            return
        a, y = at[PARENT[len(at)]]
        for nxt in ((1 - a, y), (a, (y + 1) % NY), (a, (y - 1) % NY)):
            if nxt not in at:
                grow(at + [nxt])

    grow([(0, 0)])
    return found


def move(at, by):
    return ((at[0] + by[0]) % 2, (at[1] + by[1]) % NY)


@functools.cache
def plan():
    shapes = embeddings()
    pairs = {(h, e): [] for h in range(2) for e in range(1, 8)}
    where = [dict() for _ in range(NDEV)]
    for z in range(NZ):
        choice = iter(EMBED[z])
        for core in range(NCORE):
            col = z * NCORE + core
            for a in range(2):
                for y in range(NY):
                    if (col - LOCAL * (a * NY + y)) % NCOL >= LOCAL:
                        continue
                    for h in range(2):
                        spots = [move(p, (a, y)) for p in shapes[next(choice)]]
                        for g in range(2):
                            first = LOCAL * ((2 * g + a) * NY + y)
                            block = first + (col - first) % NCOL
                            ids = [dev(2 * g + p[0], p[1], z, core) for p in spots]
                            for e in range(8):
                                where[ids[e]].setdefault(block, [0, 0])[h] = e
                                if e:
                                    pairs[h, e].append((ids[PARENT[e]], ids[e]))
    rows = []
    blocks = []
    for d in range(NDEV):
        blocks.append(sorted(where[d], key=lambda b: (max(where[d][b]), b)))
    for d in range(NDEV):
        row, col = d // NCOL, d % NCOL
        x, y = row // NY, row % NY
        z, core = col // NCORE, col % NCORE
        mate_row = (NX - 1 - x) * NY + y
        mate = mate_row * NCOL + col
        first = LOCAL * row
        j = (col - first) % NCOL
        q = (z % 2) * 2 + core
        order = [q, q + 4, q ^ 2, (q ^ 2) + 4, q ^ 1, (q ^ 1) + 4, q ^ 3, (q ^ 3) + 4]
        mine = blocks[d]
        rows.append(
            [min(j, LOCAL - 1), q, first, LOCAL * mate_row]
            + order
            + [where[d][b][0] for b in mine]
            + [where[d][b][1] for b in mine]
            + [b // NCOL for b in mine]
            + [b // NCOL for b in blocks[mate]]
            + mine
        )
    return pairs, np.asarray(rows, np.int32)


T_SEND, T_Q, T_FIRST, T_MATE, T_ORDER, T_SEL, T_SLOT, T_MSLOT, T_BLOCK = 0, 1, 2, 3, 4, 12, 22, 27, 32


def shifted(dz=0, dcore=0):
    return [
        (dev(x, y, z, k), dev(x, y, (z + dz) % NZ, (k + dcore) % NCORE))
        for x in range(NX)
        for y in range(NY)
        for z in range(NZ)
        for k in range(NCORE)
    ]


def mates():
    return [(dev(x, y, z, k), dev(NX - 1 - x, y, z, k)) for x in range(NX) for y in range(NY) for z in range(NZ) for k in range(NCORE)]


def spread(x_ref, wide):
    for side, ref in enumerate(wide):
        values = x_ref[:, :, side * 128 : (side + 1) * 128]
        ref[...] = values.astype(jnp.float32).reshape(ref.shape)


def pick(wide, p, stride, inside):
    rows = jnp.concatenate([ref[pl.ds(p, BLK, stride=stride), :] for ref in wide], axis=1)
    return jnp.where(inside, rows, 0.0).astype(jnp.bfloat16)


def inside_of(start, end):
    orbital = lax.broadcasted_iota(jnp.int32, (BLK, OCC), 1)
    return (orbital >= start) & (orbital < end)


def send_kernel(tab, start, end, x_ref, out_ref, *wide):
    block = tab[T_FIRST] + tab[T_SEND]
    inside = inside_of(start[block], end[block])
    spread(x_ref, wide)
    for p in range(16):
        out_ref[p // 4, :, (p % 4) * OCC : (p % 4 + 1) * OCC] = pick(wide, p, 16, inside)


def send_half(scalars, coefficients, half):
    return pl.pallas_call(
        send_kernel,
        grid_spec=pltpu.PrefetchScalarGridSpec(
            num_scalar_prefetch=3,
            grid=(1,),
            in_specs=[pl.BlockSpec((BLK, 16, OCC), lambda i, tab, s, e: (tab[T_SEND], half, 0))],
            out_specs=pl.BlockSpec((4, BLK, SLW), lambda i, tab, s, e: (0, 0, 0)),
            scratch_shapes=[pltpu.VMEM((BLK * 16, 128), jnp.float32)] * 2,
        ),
        out_shape=jax.ShapeDtypeStruct((4, BLK, SLW), jnp.bfloat16),
        compiler_params=pltpu.CompilerParams(vmem_limit_bytes=32 << 20),
        cost_estimate=pl.CostEstimate(flops=0, bytes_accessed=4 << 20, transcendentals=0),
        name="send_half",
    )(*scalars, coefficients)


def rows_kernel(tab, start, end, x_ref, out_ref, *wide):
    block = tab[T_FIRST] + pl.program_id(0)
    inside = inside_of(start[block], end[block])
    spread(x_ref, wide)
    for p in range(16):
        out_ref[p // 4, :, (p % 4) * OCC : (p % 4 + 1) * OCC] = pick(wide, p, 16, inside)


def own_rows(scalars, coefficients):
    return pl.pallas_call(
        rows_kernel,
        grid_spec=pltpu.PrefetchScalarGridSpec(
            num_scalar_prefetch=3,
            grid=(LOCAL, 2),
            in_specs=[pl.BlockSpec((BLK, 16, OCC), lambda i, g, tab, s, e: (i, g, 0))],
            out_specs=pl.BlockSpec((4, BLK, SLW), lambda i, g, tab, s, e: (g, i, 0)),
            scratch_shapes=[pltpu.VMEM((BLK * 16, 128), jnp.float32)] * 2,
        ),
        out_shape=jax.ShapeDtypeStruct((NSL, ROWS, SLW), jnp.bfloat16),
        compiler_params=pltpu.CompilerParams(vmem_limit_bytes=32 << 20),
        cost_estimate=pl.CostEstimate(flops=0, bytes_accessed=20 << 20, transcendentals=0),
        name="own_rows",
    )(*scalars, coefficients)


def parts_kernel(tab, start, end, x_ref, low_ref, high_ref, *wide):
    block = tab[T_FIRST] + pl.program_id(0)
    inside = inside_of(start[block], end[block])
    spread(x_ref, wide)
    for m in range(4):
        p = 4 * tab[T_Q] + m
        low_ref[:, m * OCC : (m + 1) * OCC] = pick(wide, p, NAUX, inside)
        high_ref[:, m * OCC : (m + 1) * OCC] = pick(wide, p + 16, NAUX, inside)


def mate_parts(scalars, coefficients):
    part = jax.ShapeDtypeStruct((ROWS, SLW), jnp.bfloat16)
    return pl.pallas_call(
        parts_kernel,
        grid_spec=pltpu.PrefetchScalarGridSpec(
            num_scalar_prefetch=3,
            grid=(LOCAL,),
            in_specs=[pl.BlockSpec((BLK, NAUX, OCC), lambda i, tab, s, e: (i, 0, 0))],
            out_specs=[pl.BlockSpec((BLK, SLW), lambda i, tab, s, e: (i, 0))] * 2,
            scratch_shapes=[pltpu.VMEM((BLK * NAUX, 128), jnp.float32)] * 2,
        ),
        out_shape=[part, part],
        compiler_params=pltpu.CompilerParams(vmem_limit_bytes=32 << 20),
        cost_estimate=pl.CostEstimate(flops=0, bytes_accessed=13 << 20, transcendentals=0),
        name="mate_parts",
    )(*scalars, coefficients)


def product_kernel(positions, nodes, mate, n_left, tab, flags, *refs):
    left = refs[:n_left]
    cand = refs[n_left : n_left + 2 * nodes]
    out_ref, lhs, rhs, acc, left_sem, right_sem = refs[n_left + 2 * nodes :]
    n = len(positions)
    for i, k in enumerate(positions):
        for h in range(2):
            target = rhs.at[pl.ds(4 * h, 4), pl.ds(i * BLK, BLK), :]
            for e in range(nodes):

                @pl.when(tab[T_SEL + 5 * h + k] == e)
                def _(h=h, e=e, target=target, i=i):
                    pltpu.make_async_copy(cand[h * nodes + e], target, right_sem.at[i, h]).start()

    def left_copy(s):
        source = left[s] if n_left == NSL else left[0].at[s]
        return pltpu.make_async_copy(source, lhs.at[s], left_sem.at[s])

    for s in range(NSL):
        left_copy(s).start()
    for i in range(n):
        for h in range(2):
            target = rhs.at[pl.ds(4 * h, 4), pl.ds(i * BLK, BLK), :]
            pltpu.make_async_copy(cand[h * nodes], target, right_sem.at[i, h]).wait()
    for s in range(NSL):
        left_copy(s).wait()
        where = tab[T_ORDER + s] if mate else s
        term = lax.dot_general(lhs[s], rhs[where], (((1,), (1,)), ((), ())), preferred_element_type=jnp.float32)
        if s == 0:
            acc[...] = term
        else:
            acc[...] += term
    base = 25 if mate else 0
    for i, k in enumerate(positions):
        for a in range(LOCAL):
            weight = flags[base + LOCAL * k + a].astype(jnp.float32)
            out_ref[i, a * BLK : (a + 1) * BLK, :] = acc[a * BLK : (a + 1) * BLK, i * BLK : (i + 1) * BLK] * weight


def products(tab, flags, left, cand, positions, mate):
    nodes = len(cand[0])
    n = len(positions)
    anywhere = pl.BlockSpec(memory_space=pl.ANY)
    return pl.pallas_call(
        functools.partial(product_kernel, positions, nodes, mate, len(left)),
        grid_spec=pltpu.PrefetchScalarGridSpec(
            num_scalar_prefetch=2,
            grid=(1,),
            in_specs=[anywhere] * (len(left) + 2 * nodes),
            out_specs=pl.BlockSpec((n, ROWS, BLK), lambda i, tab, flags: (0, 0, 0)),
            scratch_shapes=[
                pltpu.VMEM((NSL, ROWS, SLW), jnp.bfloat16),
                pltpu.VMEM((NSL, n * BLK, SLW), jnp.bfloat16),
                pltpu.VMEM((ROWS, n * BLK), jnp.float32),
                pltpu.SemaphoreType.DMA((NSL,)),
                pltpu.SemaphoreType.DMA((n, 2)),
            ],
        ),
        out_shape=jax.ShapeDtypeStruct((n, ROWS, BLK), jnp.float32),
        compiler_params=pltpu.CompilerParams(vmem_limit_bytes=40 << 20),
        cost_estimate=pl.CostEstimate(
            flops=2 * ROWS * n * BLK * NSL * SLW, bytes_accessed=(10 + 2 * n) << 20, transcendentals=0
        ),
        name="products",
    )(tab, flags, *left, *cand[0], *cand[1])


def place_kernel(tab, *refs):
    *parts, out_ref = refs
    half = len(parts) // 2
    for side in range(2):
        base = T_MSLOT if side else T_SLOT
        for ref, positions in zip(parts[side * half : (side + 1) * half], GROUPS):
            for i, k in enumerate(positions):
                out_ref[pl.ds(tab[base + k], BLK, stride=10), :] = ref[i]


def place(tab, own, got):
    specs = [pl.BlockSpec((len(g), BLK, BLK), lambda i, tab: (0, i, 0)) for g in GROUPS]
    return pl.pallas_call(
        place_kernel,
        grid_spec=pltpu.PrefetchScalarGridSpec(
            num_scalar_prefetch=1,
            grid=(LOCAL,),
            in_specs=specs + specs,
            out_specs=pl.BlockSpec((BLK * 10, BLK), lambda i, tab: (i, 0)),
        ),
        out_shape=jax.ShapeDtypeStruct((ROWS * 10, BLK), jnp.float32),
        cost_estimate=pl.CostEstimate(flops=0, bytes_accessed=7 << 20, transcendentals=0),
        name="place",
    )(tab, *own, *got)


def listed_flags(pair_list, tab):
    first = jnp.min(pair_list, axis=1)
    second = jnp.max(pair_list, axis=1)
    codes = first * 256 + second
    heads = jnp.stack([tab[T_FIRST], tab[T_MATE]])
    a = heads[:, None, None] + jnp.arange(LOCAL, dtype=jnp.int32)[None, None, :]
    b = tab[T_BLOCK : T_BLOCK + 5][None, :, None]
    wanted = (jnp.minimum(a, b) * 256 + jnp.maximum(a, b)).reshape(-1)
    return jnp.any(codes[None, :] == wanted[:, None], axis=1).astype(jnp.int32)


def per_device(coefficients, range_start, range_end, pair_list):
    pairs, table = plan()
    here = lax.axis_index("row") * NCOL + lax.axis_index("col")
    tab = lax.dynamic_index_in_dim(jnp.asarray(table), here, 0, keepdims=False)
    scalars = (tab, range_start, range_end)

    roots = [send_half(scalars, coefficients, h) for h in range(2)]
    low, high = mate_parts(scalars, coefficients)
    held = {(h, 0): roots[h] for h in range(2)}
    for h, e in ORDER:
        held[h, e] = lax.ppermute(held[h, PARENT[e]], AXES, pairs[h, e])
    far = [lax.ppermute(v, AXES, mates()) for v in (low, high)]
    far += [lax.ppermute(far[0], AXES, shifted(dz=-1)), lax.ppermute(far[1], AXES, shifted(dz=1))]
    far += [lax.ppermute(v, AXES, shifted(dcore=1)) for v in far]

    flags = listed_flags(pair_list, tab)
    rows = own_rows(scalars, coefficients)
    own, got = [], []
    for positions, last in zip(GROUPS, REACH):
        cand = [[held[h, e] for e in range(last + 1)] for h in range(2)]
        sent = products(tab, flags, far, cand, positions, True)
        got.append(lax.ppermute(sent, AXES, mates()))
        own.append(products(tab, flags, [rows], cand, positions, False))
    return place(tab, own, got).reshape(ROWS, 10, 1, BLK)


def solution(mesh):
    in_specs = (P("row", None, None), P(), P(), P())
    out_specs = P("row", None, "col", None)
    return jax.shard_map(per_device, mesh=mesh, in_specs=in_specs, out_specs=out_specs, check_vma=False)
```

```python
import functools

import jax
import jax.numpy as jnp
from jax import lax
from jax.experimental import pallas as pl
from jax.experimental.pallas import tpu as pltpu
from jax.sharding import PartitionSpec as P

BLK = 128
NROW, NCOL = 16, 8
LOCAL = 5
ROWS = LOCAL * BLK
NAUX, OCC = 32, 256
WIDTH = NAUX * OCC
PART = BLK // NCOL
NSL = 8
SLW = WIDTH // NSL
SLOTS = LOCAL * NROW // NCOL


def source(col, j):
    return 5 * (col - j + 8) % 8


def masked(x, start, end):
    orbital = lax.broadcasted_iota(jnp.int32, x.shape, 2)
    inside = (orbital >= start) & (orbital < end)
    return jnp.where(inside, x.astype(jnp.float32), 0.0).astype(jnp.bfloat16)


def part_kernel(where, start, end, x_ref, *out_refs):
    i = pl.program_id(0)
    block = LOCAL * where[0] + i
    values = masked(x_ref[...], start[block], end[block]).reshape(PART, WIDTH)
    for j, ref in enumerate(out_refs):

        @pl.when(i == j)
        def _(ref=ref):
            ref[...] = values


def own_part(scalars, coefficients):
    return pl.pallas_call(
        part_kernel,
        grid_spec=pltpu.PrefetchScalarGridSpec(
            num_scalar_prefetch=3,
            grid=(LOCAL,),
            in_specs=[pl.BlockSpec((PART, NAUX, OCC), lambda i, w, s, e: (NCOL * i + w[1], 0, 0))],
            out_specs=[pl.BlockSpec((PART, WIDTH), lambda i, w, s, e: (0, 0))] * LOCAL,
        ),
        out_shape=[jax.ShapeDtypeStruct((PART, WIDTH), jnp.bfloat16)] * LOCAL,
        compiler_params=pltpu.CompilerParams(vmem_limit_bytes=32 << 20),
        cost_estimate=pl.CostEstimate(flops=0, bytes_accessed=5 << 19, transcendentals=0),
        name="own_part",
    )(*scalars, coefficients)


def rows_kernel(where, start, end, x_ref, out_ref):
    block = LOCAL * where[0] + pl.program_id(0)
    values = masked(x_ref[...], start[block], end[block]).reshape(BLK, 16 * OCC)
    for s in range(4):
        out_ref[s] = values[:, s * SLW : (s + 1) * SLW]


def own_rows(scalars, coefficients):
    return pl.pallas_call(
        rows_kernel,
        grid_spec=pltpu.PrefetchScalarGridSpec(
            num_scalar_prefetch=3,
            grid=(LOCAL, 2),
            in_specs=[pl.BlockSpec((BLK, 16, OCC), lambda i, g, w, s, e: (i, g, 0))],
            out_specs=pl.BlockSpec((4, BLK, SLW), lambda i, g, w, s, e: (g, i, 0)),
        ),
        out_shape=jax.ShapeDtypeStruct((NSL, ROWS, SLW), jnp.bfloat16),
        compiler_params=pltpu.CompilerParams(vmem_limit_bytes=32 << 20),
        cost_estimate=pl.CostEstimate(flops=0, bytes_accessed=20 << 20, transcendentals=0),
        name="own_rows",
    )(*scalars, coefficients)


def product_kernel(j, gathered, rows, out_ref, left, right, acc, left_sem, right_sem):
    def copies(s):
        span = pl.ds(s * SLW, SLW)
        return (
            pltpu.make_async_copy(gathered.at[:, span], left.at[s], left_sem.at[s]),
            pltpu.make_async_copy(rows.at[s], right.at[s], right_sem.at[s]),
        )

    for s in range(NSL):
        for copy in copies(s):
            copy.start()
    for s in range(NSL):
        for copy in copies(s):
            copy.wait()
        term = lax.dot_general(left[s], right[s], (((1,), (1,)), ((), ())), preferred_element_type=jnp.float32)
        if s == 0:
            acc[...] = term
        else:
            acc[...] += term
    for col in range(NCOL):
        for h in range(2):
            first = (source(col, j) + 8 * h) * PART
            out_ref[col, h * PART : (h + 1) * PART, :] = acc[first : first + PART, :]


def products(j, gathered, rows):
    anywhere = pl.BlockSpec(memory_space=pl.ANY)
    n = NROW * PART
    return pl.pallas_call(
        functools.partial(product_kernel, j),
        in_specs=[anywhere, anywhere],
        out_specs=pl.BlockSpec(memory_space=pltpu.VMEM),
        out_shape=jax.ShapeDtypeStruct((NCOL, 2 * PART, ROWS), jnp.float32),
        scratch_shapes=[
            pltpu.VMEM((NSL, n, SLW), jnp.bfloat16),
            pltpu.VMEM((NSL, ROWS, SLW), jnp.bfloat16),
            pltpu.VMEM((n, ROWS), jnp.float32),
            pltpu.SemaphoreType.DMA((NSL,)),
            pltpu.SemaphoreType.DMA((NSL,)),
        ],
        compiler_params=pltpu.CompilerParams(vmem_limit_bytes=40 << 20),
        cost_estimate=pl.CostEstimate(flops=2 * n * ROWS * WIDTH, bytes_accessed=15 << 20, transcendentals=0),
        name="products",
    )(gathered, rows)


def place_kernel(where, flags, *refs):
    *pieces, out_ref = refs
    k = pl.program_id(0)
    col = where[1]
    for j, ref in enumerate(pieces):
        first = lax.rem(5 * (col - j + 8), 8)
        for h in range(2):
            slot = lax.div(LOCAL * first + j, NCOL) + LOCAL * h
            tile = ref[:, h * PART : (h + 1) * PART, :].reshape(BLK, BLK)
            weight = flags[SLOTS * k + slot].astype(jnp.float32)
            out_ref[pl.ds(slot, BLK, stride=SLOTS), :] = tile.T * weight


def place(where, flags, pieces):
    return pl.pallas_call(
        place_kernel,
        grid_spec=pltpu.PrefetchScalarGridSpec(
            num_scalar_prefetch=2,
            grid=(LOCAL,),
            in_specs=[pl.BlockSpec((NCOL, 2 * PART, BLK), lambda i, w, f: (0, 0, i))] * LOCAL,
            out_specs=pl.BlockSpec((BLK * SLOTS, BLK), lambda i, w, f: (i, 0)),
        ),
        out_shape=jax.ShapeDtypeStruct((ROWS * SLOTS, BLK), jnp.float32),
        compiler_params=pltpu.CompilerParams(vmem_limit_bytes=32 << 20),
        cost_estimate=pl.CostEstimate(flops=0, bytes_accessed=7 << 20, transcendentals=0),
        name="place",
    )(where, flags, *pieces)


def listed_flags(pair_list, row, col):
    first = jnp.min(pair_list, axis=1)
    second = jnp.max(pair_list, axis=1)
    codes = first * 256 + second
    a = LOCAL * row + jnp.arange(LOCAL, dtype=jnp.int32)[:, None]
    b = col + NCOL * jnp.arange(SLOTS, dtype=jnp.int32)[None, :]
    wanted = (jnp.minimum(a, b) * 256 + jnp.maximum(a, b)).reshape(-1)
    return jnp.any(codes[None, :] == wanted[:, None], axis=1).astype(jnp.int32)


def per_device(coefficients, range_start, range_end, pair_list):
    row, col = lax.axis_index("row"), lax.axis_index("col")
    where = jnp.stack([row, col]).astype(jnp.int32)
    scalars = (where, range_start, range_end)
    parts = own_part(scalars, coefficients)
    gathered = [lax.all_gather(part, "row", axis=0, tiled=True) for part in parts]
    rows = own_rows(scalars, coefficients)
    flags = listed_flags(pair_list, row, col)
    pieces = [
        lax.all_to_all(products(j, g, rows), "col", 0, 0, tiled=True) for j, g in enumerate(gathered)
    ]
    return place(where, flags, pieces).reshape(ROWS, SLOTS, 1, BLK)


def solution(mesh):
    in_specs = (P("row", None, None), P(), P(), P())
    out_specs = P("row", None, "col", None)
    return jax.shard_map(per_device, mesh=mesh, in_specs=in_specs, out_specs=out_specs, check_vma=False)
```

```python
import functools

import jax
import jax.numpy as jnp
import numpy as np
from jax import lax
from jax.experimental import pallas as pl
from jax.experimental.pallas import tpu as pltpu
from jax.sharding import PartitionSpec as P

BLK = 128
NX, NY, NZ, NCORE = 4, 4, 4, 2
NCOL = NZ * NCORE
NDEV = NX * NY * NCOL
LOCAL = 5
ROWS = LOCAL * BLK
NAUX, OCC = 32, 256
WIDTH = NAUX * OCC
PIECE = BLK // NCOL
PART = LOCAL * PIECE
NSL = 8
SLW = WIDTH // NSL
SLOTS = LOCAL * NX * NY // NCOL
AXES = ("row", "col")

UNITS = (
    ((0, 0), (0, 0), None),
    ((0, 1), (1, 0), (0, 0)),
    ((1, 0), (0, 1), (0, 0)),
    ((3, 0), (3, 0), (0, 0)),
    ((0, 3), (0, 3), (0, 0)),
    ((1, 1), (1, 1), (1, 1)),
    ((2, 0), (2, 0), (3, 3)),
    ((1, 3), (1, 3), (2, 1)),
    ((2, 1), (2, 1), (5, 5)),
    ((1, 2), (1, 2), (5, 5)),
    ((0, 2), (2, 2), (4, 8)),
    ((2, 2), (0, 2), (9, 9)),
)
BACK = (5, 7, 8, 9)
GROUPS = ((0, 1, 2, 3, 4), (5,), (6, 7), (8, 9), (10, 11))
BATCHES = (
    (("U", 0), ("U", 1), ("U", 2), ("U", 4), ("U", 5), ("V", 5)),
    (("U", 3), ("U", 6), ("U", 7), ("V", 7), ("U", 8), ("U", 9)),
    (("U", 10), ("U", 11), ("V", 8), ("V", 9)),
)
ENTRIES = tuple(entry for batch in BATCHES for entry in batch)


def dev(x, y, col):
    return (x * NY + y) * NCOL + col


def shifted(moves):
    return [
        (dev(x, y, col), dev((x + moves[col % 2][0]) % NX, (y + moves[col % 2][1]) % NY, col))
        for x in range(NX)
        for y in range(NY)
        for col in range(NCOL)
    ]


def step_to(unit):
    moves = []
    for core in range(NCORE):
        here, there = UNITS[unit][core], UNITS[UNITS[unit][2][core]][core]
        moves.append(((here[0] - there[0]) % NX, (here[1] - there[1]) % NY))
    return moves


def step_back(unit):
    return [(-UNITS[unit][core][0] % NX, -UNITS[unit][core][1] % NY) for core in range(NCORE)]


def other_row(kind, unit, core, x, y):
    m = UNITS[unit][core]
    sign = -1 if kind == "U" else 1
    return (x + sign * m[0]) % NX * NY + (y + sign * m[1]) % NY


@functools.cache
def tables():
    sizes = []
    filled = {}
    for n, batch in enumerate(BATCHES):
        for x in range(NX):
            for y in range(NY):
                for core in range(NCORE):
                    classes = {c: [] for c in range(NCOL)}
                    for kind, unit in batch:
                        row = other_row(kind, unit, core, x, y)
                        for block in range(LOCAL * row, LOCAL * row + LOCAL):
                            classes[block % NCOL].append((block, kind))
                    filled[x, y, n, core] = {c: sorted(v) for c, v in classes.items()}
                assert filled[x, y, n, 0] == filled[x, y, n, 1]
        sizes.append(max(len(v) for k, f in filled.items() if k[2] == n for v in f.values()))
    rows = []
    for x in range(NX):
        for y in range(NY):
            for col in range(NCOL):
                values = [x * NY + y, col]
                for n, batch in enumerate(BATCHES):
                    classes = filled[x, y, n, col % 2]
                    for kind, unit in batch:
                        row = other_row(kind, unit, col % 2, x, y)
                        for block in range(LOCAL * row, LOCAL * row + LOCAL):
                            target = block % NCOL
                            values.append(target * sizes[n] + classes[target].index((block, kind)))
                for n in range(len(BATCHES)):
                    held = filled[x, y, n, col % 2][col]
                    for slot in range(sizes[n]):
                        if slot < len(held):
                            values += [held[slot][0] // NCOL, int(held[slot][1] == "V")]
                        else:
                            values += [0, 2]
                rows.append(values)
    return tuple(sizes), np.asarray(rows, np.int32)


T_PIECES = 2
T_SLOTS = T_PIECES + LOCAL * len(ENTRIES)


def masked(x, start, end):
    orbital = lax.broadcasted_iota(jnp.int32, x.shape, 2)
    inside = (orbital >= start) & (orbital < end)
    return jnp.where(inside, x.astype(jnp.float32), 0.0).astype(jnp.bfloat16)


def part_kernel(tab, start, end, x_ref, out_ref, raw, sems):
    def fetch(j):
        return pltpu.make_async_copy(x_ref.at[pl.ds(j * BLK + tab[1] * PIECE, PIECE)], raw.at[j], sems.at[j])

    for j in range(LOCAL):
        fetch(j).start()
    for j in range(LOCAL):
        fetch(j).wait()
        block = LOCAL * tab[0] + j
        values = masked(raw[j], start[block], end[block])
        out_ref[j * PIECE : (j + 1) * PIECE, :] = values.reshape(PIECE, WIDTH)


def own_part(scalars, coefficients):
    return pl.pallas_call(
        part_kernel,
        grid_spec=pltpu.PrefetchScalarGridSpec(
            num_scalar_prefetch=3,
            grid=(1,),
            in_specs=[pl.BlockSpec(memory_space=pl.ANY)],
            out_specs=pl.BlockSpec((PART, WIDTH), lambda i, t, s, e: (0, 0)),
            scratch_shapes=[pltpu.VMEM((LOCAL, PIECE, NAUX, OCC), jnp.bfloat16), pltpu.SemaphoreType.DMA((LOCAL,))],
        ),
        out_shape=jax.ShapeDtypeStruct((PART, WIDTH), jnp.bfloat16),
        compiler_params=pltpu.CompilerParams(vmem_limit_bytes=56 << 20),
        cost_estimate=pl.CostEstimate(flops=0, bytes_accessed=5 << 19, transcendentals=0),
        name="own_part",
    )(*scalars, coefficients)


def rows_kernel(tab, start, end, x_ref, out_ref):
    block = LOCAL * tab[0] + pl.program_id(0)
    values = masked(x_ref[...], start[block], end[block]).reshape(BLK, 16 * OCC)
    for s in range(4):
        out_ref[s] = values[:, s * SLW : (s + 1) * SLW]


def own_rows(scalars, coefficients):
    return pl.pallas_call(
        rows_kernel,
        grid_spec=pltpu.PrefetchScalarGridSpec(
            num_scalar_prefetch=3,
            grid=(LOCAL, 2),
            in_specs=[pl.BlockSpec((BLK, 16, OCC), lambda i, g, t, s, e: (i, g, 0))],
            out_specs=pl.BlockSpec((4, BLK, SLW), lambda i, g, t, s, e: (g, i, 0)),
        ),
        out_shape=jax.ShapeDtypeStruct((NSL, ROWS, SLW), jnp.bfloat16),
        compiler_params=pltpu.CompilerParams(vmem_limit_bytes=56 << 20),
        cost_estimate=pl.CostEstimate(flops=0, bytes_accessed=20 << 20, transcendentals=0),
        name="own_rows",
    )(*scalars, coefficients)


def product_kernel(n, *refs):
    parts, rows, outs = refs[:n], refs[n], refs[n + 1 : 2 * n + 1]
    left, right, acc, left_sem, right_sem = refs[2 * n + 1 :]

    def copies(s):
        span = pl.ds(s * SLW, SLW)
        found = [pltpu.make_async_copy(rows.at[s], right.at[s], right_sem.at[s])]
        for i, part in enumerate(parts):
            target = left.at[s, pl.ds(i * PART, PART), :]
            found.append(pltpu.make_async_copy(part.at[:, span], target, left_sem.at[i, s]))
        return found

    for s in range(NSL):
        for copy in copies(s):
            copy.start()
    for s in range(NSL):
        for copy in copies(s):
            copy.wait()
        term = lax.dot_general(left[s], right[s], (((1,), (1,)), ((), ())), preferred_element_type=jnp.float32)
        if s == 0:
            acc[...] = term
        else:
            acc[...] += term
    for i, out in enumerate(outs):
        out[...] = acc[i * PART : (i + 1) * PART, :]


def products(parts, rows):
    n = len(parts)
    anywhere = pl.BlockSpec(memory_space=pl.ANY)
    return pl.pallas_call(
        functools.partial(product_kernel, n),
        grid=(1,),
        in_specs=[anywhere] * (n + 1),
        out_specs=[pl.BlockSpec((PART, ROWS), lambda i: (0, 0))] * n,
        out_shape=[jax.ShapeDtypeStruct((PART, ROWS), jnp.float32)] * n,
        scratch_shapes=[
            pltpu.VMEM((NSL, n * PART, SLW), jnp.bfloat16),
            pltpu.VMEM((NSL, ROWS, SLW), jnp.bfloat16),
            pltpu.VMEM((n * PART, ROWS), jnp.float32),
            pltpu.SemaphoreType.DMA((n, NSL)),
            pltpu.SemaphoreType.DMA((NSL,)),
        ],
        compiler_params=pltpu.CompilerParams(vmem_limit_bytes=56 << 20),
        cost_estimate=pl.CostEstimate(
            flops=2 * n * PART * ROWS * WIDTH, bytes_accessed=(10 << 20) + n * (3 << 19), transcendentals=0
        ),
        name="products",
    )(*parts, rows)


def pack_kernel(first, batch, tab, *refs):
    *parts, out_ref = refs
    for n, (kind, _) in enumerate(batch):
        part = parts[n]
        for j in range(LOCAL):
            where = tab[T_PIECES + LOCAL * (first + n) + j]
            if kind == "V":
                out_ref[where] = part[:, j * BLK : (j + 1) * BLK]
                continue
            for k in range(LOCAL):
                piece = part[j * PIECE : (j + 1) * PIECE, k * BLK : (k + 1) * BLK]
                out_ref[where, k * PIECE : (k + 1) * PIECE, :] = piece


def pack(tab, first, batch, size, parts):
    return pl.pallas_call(
        functools.partial(pack_kernel, first, batch),
        grid_spec=pltpu.PrefetchScalarGridSpec(
            num_scalar_prefetch=1,
            grid=(1,),
            in_specs=[pl.BlockSpec((PART, ROWS), lambda i, t: (0, 0))] * len(parts),
            out_specs=pl.BlockSpec((NCOL * size, PART, BLK), lambda i, t: (0, 0, 0)),
        ),
        out_shape=jax.ShapeDtypeStruct((NCOL * size, PART, BLK), jnp.float32),
        compiler_params=pltpu.CompilerParams(vmem_limit_bytes=20 << 20),
        cost_estimate=pl.CostEstimate(flops=0, bytes_accessed=3 << 20, transcendentals=0),
        name="pack",
    )(tab, *parts)


def place_kernel(sizes, tab, flags, *refs):
    *pieces, out_ref = refs
    k = pl.program_id(0)
    at = T_SLOTS
    for ref, size in zip(pieces, sizes):
        for n in range(size):
            slot, kind = tab[at], tab[at + 1]
            at += 2
            weight = flags[SLOTS * k + slot].astype(jnp.float32)

            @pl.when(kind == 0)
            def _(ref=ref, n=n, slot=slot, weight=weight):
                tile = ref[:, n].reshape(BLK, BLK)
                out_ref[pl.ds(slot, BLK, stride=SLOTS), :] = tile.T * weight

            @pl.when(kind == 1)
            def _(ref=ref, n=n, slot=slot, weight=weight):
                tile = ref[:, n].reshape(BLK, BLK)
                out_ref[pl.ds(slot, BLK, stride=SLOTS), :] = tile * weight


def place(tab, flags, sizes, pieces):
    return pl.pallas_call(
        functools.partial(place_kernel, sizes),
        grid_spec=pltpu.PrefetchScalarGridSpec(
            num_scalar_prefetch=2,
            grid=(LOCAL,),
            in_specs=[pl.BlockSpec((NCOL, size, PIECE, BLK), lambda i, t, f: (0, 0, i, 0)) for size in sizes],
            out_specs=pl.BlockSpec((BLK * SLOTS, BLK), lambda i, t, f: (i, 0)),
        ),
        out_shape=jax.ShapeDtypeStruct((ROWS * SLOTS, BLK), jnp.float32),
        compiler_params=pltpu.CompilerParams(vmem_limit_bytes=20 << 20),
        cost_estimate=pl.CostEstimate(flops=0, bytes_accessed=7 << 20, transcendentals=0),
        name="place",
    )(tab, flags, *pieces)


def listed_flags(pair_list, row, col):
    first = jnp.min(pair_list, axis=1)
    second = jnp.max(pair_list, axis=1)
    codes = first * 256 + second
    a = LOCAL * row + jnp.arange(LOCAL, dtype=jnp.int32)[:, None]
    b = col + NCOL * jnp.arange(SLOTS, dtype=jnp.int32)[None, :]
    wanted = (jnp.minimum(a, b) * 256 + jnp.maximum(a, b)).reshape(-1)
    return jnp.any(codes[None, :] == wanted[:, None], axis=1).astype(jnp.int32)


def per_device(coefficients, range_start, range_end, pair_list):
    sizes, table = tables()
    row, col = lax.axis_index("row"), lax.axis_index("col")
    tab = lax.dynamic_index_in_dim(jnp.asarray(table), row * NCOL + col, 0, keepdims=False)
    scalars = (tab, range_start, range_end)
    held = {0: own_part(scalars, coefficients)}
    rows = own_rows(scalars, coefficients)
    flags = listed_flags(pair_list, row, col)
    made = {}

    def send(unit, *first):
        a, b = UNITS[unit][2]
        source = held[a] if a == b else jnp.where(col % 2 == 0, held[a], held[b])
        if first:
            source = lax.optimization_barrier((source, *first))[0]
        held[unit] = lax.ppermute(source, AXES, shifted(step_to(unit)))

    def multiply(group):
        for unit, product in zip(group, products([held[u] for u in group], rows)):
            made["U", unit] = product
            if unit in BACK:
                made["V", unit] = lax.ppermute(product, AXES, shifted(step_back(unit)))

    for unit in (1, 2, 3, 4):
        send(unit)
    for unit in (5, 6, 7):
        send(unit, rows)
    multiply(GROUPS[0])
    send(8, made["U", 0])
    send(9, made["U", 0])
    send(11)
    send(10)
    for group in GROUPS[1:]:
        multiply(group)
    pieces = []
    first = 0
    for batch, size in zip(BATCHES, sizes):
        message = pack(tab, first, batch, size, [made[entry] for entry in batch])
        first += len(batch)
        got = lax.all_to_all(message, "col", 0, 0, tiled=True)
        pieces.append(got.reshape(NCOL, size, PART, BLK))
    return place(tab, flags, sizes, pieces).reshape(ROWS, SLOTS, 1, BLK)


def solution(mesh):
    in_specs = (P("row", None, None), P(), P(), P())
    out_specs = P("row", None, "col", None)
    return jax.shard_map(per_device, mesh=mesh, in_specs=in_specs, out_specs=out_specs, check_vma=False)
```

```python
import functools

import jax
import jax.numpy as jnp
import numpy as np
from jax import lax
from jax.experimental import pallas as pl
from jax.experimental.pallas import tpu as pltpu
from jax.sharding import PartitionSpec as P

BLK = 128
NX, NY, NZ, NCORE = 4, 4, 4, 2
NCOL = NZ * NCORE
NDEV = NX * NY * NCOL
LOCAL = 5
ROWS = LOCAL * BLK
NAUX, OCC = 32, 256
WIDTH = NAUX * OCC
PIECE = BLK // NCOL
PART = LOCAL * PIECE
NSL = 8
SLW = WIDTH // NSL
SLOTS = LOCAL * NX * NY // NCOL
AXES = ("row", "col")

UNITS = (
    ((0, 0), (0, 0), None),
    ((0, 1), (1, 0), (0, 0)),
    ((1, 0), (0, 1), (0, 0)),
    ((3, 0), (3, 0), (0, 0)),
    ((0, 3), (0, 3), (0, 0)),
    ((1, 1), (1, 1), (1, 1)),
    ((2, 0), (2, 0), (3, 3)),
    ((1, 3), (1, 3), (2, 1)),
    ((2, 1), (2, 1), (5, 5)),
    ((1, 2), (1, 2), (5, 5)),
    ((0, 2), (2, 2), (4, 8)),
    ((2, 2), (0, 2), (9, 9)),
)
BACK = (5, 7, 8, 9)
GROUPS = ((0, 1, 2, 3, 4), (5,), (6, 7), (8, 9), (10, 11))
BATCHES = (
    (("U", 0), ("U", 1), ("U", 2), ("U", 3), ("U", 4), ("U", 5), ("V", 5), ("U", 6), ("U", 7)),
    (("V", 7), ("U", 8), ("U", 9), ("U", 10), ("U", 11), ("V", 8), ("V", 9)),
)
ENTRIES = tuple(entry for batch in BATCHES for entry in batch)


def dev(x, y, col):
    return (x * NY + y) * NCOL + col


def shifted(moves):
    return [
        (dev(x, y, col), dev((x + moves[col % 2][0]) % NX, (y + moves[col % 2][1]) % NY, col))
        for x in range(NX)
        for y in range(NY)
        for col in range(NCOL)
    ]


def step_to(unit):
    moves = []
    for core in range(NCORE):
        here, there = UNITS[unit][core], UNITS[UNITS[unit][2][core]][core]
        moves.append(((here[0] - there[0]) % NX, (here[1] - there[1]) % NY))
    return moves


def step_back(unit):
    return [(-UNITS[unit][core][0] % NX, -UNITS[unit][core][1] % NY) for core in range(NCORE)]


def other_row(kind, unit, core, x, y):
    m = UNITS[unit][core]
    sign = -1 if kind == "U" else 1
    return (x + sign * m[0]) % NX * NY + (y + sign * m[1]) % NY


@functools.cache
def tables():
    sizes = []
    filled = {}
    for n, batch in enumerate(BATCHES):
        for x in range(NX):
            for y in range(NY):
                for core in range(NCORE):
                    classes = {c: [] for c in range(NCOL)}
                    for kind, unit in batch:
                        row = other_row(kind, unit, core, x, y)
                        for block in range(LOCAL * row, LOCAL * row + LOCAL):
                            classes[block % NCOL].append((block, kind))
                    filled[x, y, n, core] = {c: sorted(v) for c, v in classes.items()}
                assert filled[x, y, n, 0] == filled[x, y, n, 1]
        sizes.append(max(len(v) for k, f in filled.items() if k[2] == n for v in f.values()))
    rows = []
    for x in range(NX):
        for y in range(NY):
            for col in range(NCOL):
                values = [x * NY + y, col]
                for n, batch in enumerate(BATCHES):
                    classes = filled[x, y, n, col % 2]
                    for kind, unit in batch:
                        row = other_row(kind, unit, col % 2, x, y)
                        for block in range(LOCAL * row, LOCAL * row + LOCAL):
                            target = block % NCOL
                            values.append(target * sizes[n] + classes[target].index((block, kind)))
                for n in range(len(BATCHES)):
                    held = filled[x, y, n, col % 2][col]
                    for slot in range(sizes[n]):
                        if slot < len(held):
                            values += [held[slot][0] // NCOL, int(held[slot][1] == "V")]
                        else:
                            values += [0, 2]
                rows.append(values)
    return tuple(sizes), np.asarray(rows, np.int32)


T_PIECES = 2
T_SLOTS = T_PIECES + LOCAL * len(ENTRIES)


def masked(x, start, end):
    orbital = lax.broadcasted_iota(jnp.int32, x.shape, 2)
    inside = (orbital >= start) & (orbital < end)
    return jnp.where(inside, x.astype(jnp.float32), 0.0).astype(jnp.bfloat16)


def in_vmem(value):
    return pltpu.with_memory_space_constraint(value, pltpu.VMEM)


def in_hbm(value):
    return pltpu.with_memory_space_constraint(value, pltpu.HBM)


VMEM_SPEC = pl.BlockSpec(memory_space=pltpu.VMEM)
HBM_SPEC = pl.BlockSpec(memory_space=pltpu.HBM)
SMEM_SPEC = pl.BlockSpec(memory_space=pltpu.SMEM)
MARK = jax.ShapeDtypeStruct((8, 128), jnp.float32)


def part_kernel(tab, start, end, x_ref, out_ref, raw, sems):
    def fetch(j):
        return pltpu.make_async_copy(x_ref.at[pl.ds(j * BLK + tab[1] * PIECE, PIECE)], raw.at[j], sems.at[j])

    for j in range(LOCAL):
        fetch(j).start()
    for j in range(LOCAL):
        fetch(j).wait()
        block = LOCAL * tab[0] + j
        values = masked(raw[j], start[block], end[block])
        out_ref[j * PIECE : (j + 1) * PIECE, :] = values.reshape(PIECE, WIDTH)


def own_part(scalars, coefficients):
    return pl.pallas_call(
        part_kernel,
        in_specs=[SMEM_SPEC] * 3 + [HBM_SPEC],
        out_specs=VMEM_SPEC,
        out_shape=pltpu.VMEM((PART, WIDTH), jnp.bfloat16),
        scratch_shapes=[pltpu.VMEM((LOCAL, PIECE, NAUX, OCC), jnp.bfloat16), pltpu.SemaphoreType.DMA((LOCAL,))],
        compiler_params=pltpu.CompilerParams(vmem_limit_bytes=6 << 20),
        cost_estimate=pl.CostEstimate(flops=0, bytes_accessed=5 << 19, transcendentals=0),
        name="own_part",
    )(*scalars, in_hbm(coefficients))


CHUNK = 64


def rows_kernel(tab, start, end, x_ref, out_ref, mark_ref, raw, sems):
    steps = ROWS // CHUNK
    mark_ref[...] = jnp.zeros_like(mark_ref)

    def fetch(n):
        return pltpu.make_async_copy(x_ref.at[pl.ds(n * CHUNK, CHUNK)], raw.at[lax.rem(n, 4)], sems.at[lax.rem(n, 4)])

    for n in range(3):
        fetch(n).start()

    def step(n, carry):
        @pl.when(n + 3 < steps)
        def _():
            fetch(n + 3).start()

        fetch(n).wait()
        block = LOCAL * tab[0] + lax.div(n, BLK // CHUNK)
        values = masked(raw[lax.rem(n, 4)], start[block], end[block]).reshape(CHUNK, WIDTH)
        at = pl.ds(pl.multiple_of(n * CHUNK, CHUNK), CHUNK)
        for s in range(NSL):
            out_ref[s, at, :] = values[:, s * SLW : (s + 1) * SLW]
        return carry

    lax.fori_loop(0, steps, step, 0)


def own_rows(scalars, coefficients):
    return pl.pallas_call(
        rows_kernel,
        in_specs=[SMEM_SPEC] * 3 + [HBM_SPEC],
        out_specs=[VMEM_SPEC] * 2,
        out_shape=[pltpu.VMEM((NSL, ROWS, SLW), jnp.bfloat16), MARK],
        scratch_shapes=[pltpu.VMEM((4, CHUNK, NAUX, OCC), jnp.bfloat16), pltpu.SemaphoreType.DMA((4,))],
        compiler_params=pltpu.CompilerParams(vmem_limit_bytes=12 << 20),
        cost_estimate=pl.CostEstimate(flops=0, bytes_accessed=20 << 20, transcendentals=0),
        name="own_rows",
    )(*scalars, in_hbm(coefficients))


def product_kernel(n, *refs):
    parts, rows, outs, mark_ref, acc = refs[:n], refs[n], refs[n + 2 : 2 * n + 2], refs[2 * n + 2], refs[2 * n + 3]
    mark_ref[...] = jnp.zeros_like(mark_ref)
    for s in range(NSL):
        left = jnp.concatenate([part[:, s * SLW : (s + 1) * SLW] for part in parts], axis=0)
        term = lax.dot_general(left, rows[s], (((1,), (1,)), ((), ())), preferred_element_type=jnp.float32)
        if s == 0:
            acc[...] = term
        else:
            acc[...] += term
    for i, out in enumerate(outs):
        out[...] = acc[i * PART : (i + 1) * PART, :]


def products(parts, rows, token):
    n = len(parts)
    return pl.pallas_call(
        functools.partial(product_kernel, n),
        in_specs=[VMEM_SPEC] * (n + 1) + [pl.BlockSpec(memory_space=pl.ANY)],
        out_specs=[VMEM_SPEC] * (n + 1),
        out_shape=[pltpu.VMEM((PART, ROWS), jnp.float32)] * n + [MARK],
        scratch_shapes=[pltpu.VMEM((n * PART, ROWS), jnp.float32)],
        compiler_params=pltpu.CompilerParams(vmem_limit_bytes=12 << 20),
        cost_estimate=pl.CostEstimate(
            flops=2 * n * PART * ROWS * WIDTH, bytes_accessed=(10 << 20) + n * (3 << 19), transcendentals=0
        ),
        name="products",
    )(*[in_vmem(part) for part in parts], in_vmem(rows), token)


def pack_kernel(first, batch, tab, *refs):
    *parts, _, out_ref, mark_ref = refs
    mark_ref[...] = jnp.zeros_like(mark_ref)
    for n, (kind, _) in enumerate(batch):
        part = parts[n]
        for j in range(LOCAL):
            where = tab[T_PIECES + LOCAL * (first + n) + j]
            if kind == "V":
                out_ref[where] = part[:, j * BLK : (j + 1) * BLK]
                continue
            for k in range(LOCAL):
                piece = part[j * PIECE : (j + 1) * PIECE, k * BLK : (k + 1) * BLK]
                out_ref[where, k * PIECE : (k + 1) * PIECE, :] = piece


def pack(tab, first, batch, size, parts, token):
    return pl.pallas_call(
        functools.partial(pack_kernel, first, batch),
        in_specs=[SMEM_SPEC] + [VMEM_SPEC] * len(parts) + [pl.BlockSpec(memory_space=pl.ANY)],
        out_specs=[VMEM_SPEC] * 2,
        out_shape=[pltpu.VMEM((NCOL * size, PART, BLK), jnp.float32), MARK],
        compiler_params=pltpu.CompilerParams(vmem_limit_bytes=4 << 20),
        cost_estimate=pl.CostEstimate(flops=0, bytes_accessed=3 << 20, transcendentals=0),
        name="pack",
    )(tab, *[in_vmem(part) for part in parts], token)


def place_kernel(sizes, tab, flags, *refs):
    n_in = len(sizes)
    pieces, out_ref, made, sems = refs[:n_in], refs[n_in], refs[n_in + 1], refs[n_in + 2]

    def send(k):
        return pltpu.make_async_copy(made.at[k], out_ref.at[pl.ds(k * BLK * SLOTS, BLK * SLOTS), :], sems.at[k])

    for k in range(LOCAL):
        at = T_SLOTS
        for ref, size in zip(pieces, sizes):
            for n in range(size):
                slot, kind = tab[at], tab[at + 1]
                at += 2
                weight = flags[SLOTS * k + slot].astype(jnp.float32)

                def tile(ref=ref, n=n, size=size, weight=weight):
                    found = [ref[c * size + n, k * PIECE : (k + 1) * PIECE, :] for c in range(NCOL)]
                    return jnp.concatenate(found, axis=0) * weight

                @pl.when(kind == 0)
                def _(slot=slot, tile=tile):
                    made[k, pl.ds(slot, BLK, stride=SLOTS), :] = tile().T

                @pl.when(kind == 1)
                def _(slot=slot, tile=tile):
                    made[k, pl.ds(slot, BLK, stride=SLOTS), :] = tile()

        send(k).start()
    for k in range(LOCAL):
        send(k).wait()


def place(tab, flags, sizes, pieces):
    return pl.pallas_call(
        functools.partial(place_kernel, sizes),
        in_specs=[SMEM_SPEC] * 2 + [VMEM_SPEC] * len(sizes),
        out_specs=HBM_SPEC,
        out_shape=jax.ShapeDtypeStruct((ROWS * SLOTS, BLK), jnp.float32),
        scratch_shapes=[pltpu.VMEM((LOCAL, BLK * SLOTS, BLK), jnp.float32), pltpu.SemaphoreType.DMA((LOCAL,))],
        compiler_params=pltpu.CompilerParams(vmem_limit_bytes=8 << 20),
        cost_estimate=pl.CostEstimate(flops=0, bytes_accessed=7 << 20, transcendentals=0),
        name="place",
    )(tab, flags, *[in_vmem(piece) for piece in pieces])


def flags_kernel(tab, pairs_ref, out_ref):
    first = jnp.minimum(pairs_ref[0:1, :], pairs_ref[1:2, :])
    second = jnp.maximum(pairs_ref[0:1, :], pairs_ref[1:2, :])
    codes = first * 256 + second
    for i in range(LOCAL):
        a = LOCAL * tab[0] + i
        for slot in range(SLOTS):
            b = tab[1] + NCOL * slot
            wanted = jnp.minimum(a, b) * 256 + jnp.maximum(a, b)
            out_ref[SLOTS * i + slot] = jnp.max((codes == wanted).astype(jnp.int32))


def listed_flags(tab, pair_list):
    return pl.pallas_call(
        flags_kernel,
        in_specs=[SMEM_SPEC, VMEM_SPEC],
        out_specs=SMEM_SPEC,
        out_shape=jax.ShapeDtypeStruct((LOCAL * SLOTS,), jnp.int32),
        compiler_params=pltpu.CompilerParams(vmem_limit_bytes=1 << 20),
        cost_estimate=pl.CostEstimate(flops=1 << 20, bytes_accessed=1 << 14, transcendentals=0),
        name="listed_flags",
    )(tab, pair_list.T)


def choose_kernel(tab, even_ref, odd_ref, out_ref, sem):
    core = lax.rem(tab[1], NCORE)
    for which, ref in enumerate((even_ref, odd_ref)):

        @pl.when(core == which)
        def _(ref=ref):
            pltpu.make_async_copy(ref, out_ref, sem).start()

    pltpu.make_async_copy(even_ref, out_ref, sem).wait()


def choose(tab, even, odd):
    return pl.pallas_call(
        choose_kernel,
        in_specs=[SMEM_SPEC] + [pl.BlockSpec(memory_space=pl.ANY)] * 2,
        out_specs=VMEM_SPEC,
        out_shape=pltpu.VMEM((PART, WIDTH), jnp.bfloat16),
        scratch_shapes=[pltpu.SemaphoreType.DMA],
        compiler_params=pltpu.CompilerParams(vmem_limit_bytes=4 << 20),
        cost_estimate=pl.CostEstimate(flops=0, bytes_accessed=5 << 19, transcendentals=0),
        name="choose",
    )(tab, even, odd)


def per_device(coefficients, range_start, range_end, pair_list):
    sizes, table = tables()
    row, col = lax.axis_index("row"), lax.axis_index("col")
    tab = lax.dynamic_index_in_dim(jnp.asarray(table), row * NCOL + col, 0, keepdims=False)
    scalars = (in_hbm(tab), in_hbm(range_start), in_hbm(range_end))
    held = {0: own_part(scalars, coefficients)}
    rows, token = own_rows(scalars, coefficients)
    flags = listed_flags(tab, pair_list)
    made = {}

    def send(unit):
        a, b = UNITS[unit][2]
        source = held[a] if a == b else choose(tab, held[a], held[b])
        held[unit] = lax.ppermute(source, AXES, shifted(step_to(unit)))

    def multiply(group, token):
        *results, token = products([held[u] for u in group], rows, token)
        for unit, product in zip(group, results):
            made["U", unit] = product
            if unit in BACK:
                made["V", unit] = lax.ppermute(product, AXES, shifted(step_back(unit)))
        return token

    def gate(units, token):
        *values, token = lax.optimization_barrier((*[held[u] for u in units], token))
        held.update(zip(units, values))
        return token

    for unit in (1, 2, 3, 4):
        send(unit)
    token = gate((1, 2, 3, 4), token)
    for unit in (5, 6, 7):
        send(unit)
    token = multiply(GROUPS[0], token)
    token = gate((5,), token)
    send(8)
    send(9)
    token = multiply(GROUPS[1], token)
    token = multiply(GROUPS[2], token)
    message, token = pack(tab, 0, BATCHES[0], sizes[0], [made[entry] for entry in BATCHES[0]], token)
    pieces = [lax.all_to_all(message, "col", 0, 0, tiled=True)]
    token = gate((8, 9), token)
    send(11)
    send(10)
    token = multiply(GROUPS[3], token)
    token = multiply(GROUPS[4], token)
    message, _ = pack(tab, len(BATCHES[0]), BATCHES[1], sizes[1], [made[entry] for entry in BATCHES[1]], token)
    pieces.append(lax.all_to_all(message, "col", 0, 0, tiled=True))
    return place(tab, flags, sizes, pieces).reshape(ROWS, SLOTS, 1, BLK)


def solution(mesh):
    in_specs = (P("row", None, None), P(), P(), P())
    out_specs = P("row", None, "col", None)
    return jax.shard_map(per_device, mesh=mesh, in_specs=in_specs, out_specs=out_specs, check_vma=False)
```

```python
import functools

import jax
import jax.numpy as jnp
import numpy as np
from jax import lax
from jax.experimental import pallas as pl
from jax.experimental.pallas import tpu as pltpu
from jax.sharding import PartitionSpec as P

BLK = 128
NX, NY, NZ, NCORE = 4, 4, 4, 2
NCOL = NZ * NCORE
NDEV = NX * NY * NCOL
LOCAL = 5
ROWS = LOCAL * BLK
NAUX, OCC = 32, 256
WIDTH = NAUX * OCC
PIECE = BLK // NCOL
PART = LOCAL * PIECE
NSL = 8
SLW = WIDTH // NSL
SLOTS = LOCAL * NX * NY // NCOL
AXES = ("row", "col")

UNITS = (
    ((0, 0), (0, 0), None),
    ((0, 1), (1, 0), (0, 0)),
    ((1, 0), (0, 1), (0, 0)),
    ((3, 0), (3, 0), (0, 0)),
    ((0, 3), (0, 3), (0, 0)),
    ((1, 1), (1, 1), (1, 1)),
    ((2, 0), (2, 0), (3, 3)),
    ((1, 3), (1, 3), (2, 1)),
    ((2, 1), (2, 1), (5, 5)),
    ((1, 2), (1, 2), (5, 5)),
    ((0, 2), (2, 2), (4, 8)),
    ((2, 2), (0, 2), (9, 9)),
)
BACK = (5, 7, 8, 9)
GROUPS = ((0, 1, 2, 3, 4), (5,), (6, 7), (8, 9), (10, 11))
BATCHES = (
    (("U", 0), ("U", 1), ("U", 2), ("U", 3), ("U", 4), ("U", 5), ("V", 5), ("U", 6), ("U", 7)),
    (("V", 7), ("U", 8), ("U", 9), ("U", 10), ("U", 11), ("V", 8), ("V", 9)),
)
ENTRIES = tuple(entry for batch in BATCHES for entry in batch)


def dev(x, y, col):
    return (x * NY + y) * NCOL + col


def shifted(moves):
    return [
        (dev(x, y, col), dev((x + moves[col % 2][0]) % NX, (y + moves[col % 2][1]) % NY, col))
        for x in range(NX)
        for y in range(NY)
        for col in range(NCOL)
    ]


def step_to(unit):
    moves = []
    for core in range(NCORE):
        here, there = UNITS[unit][core], UNITS[UNITS[unit][2][core]][core]
        moves.append(((here[0] - there[0]) % NX, (here[1] - there[1]) % NY))
    return moves


def step_back(unit):
    return [(-UNITS[unit][core][0] % NX, -UNITS[unit][core][1] % NY) for core in range(NCORE)]


def other_row(kind, unit, core, x, y):
    m = UNITS[unit][core]
    sign = -1 if kind == "U" else 1
    return (x + sign * m[0]) % NX * NY + (y + sign * m[1]) % NY


@functools.cache
def tables():
    sizes = []
    filled = {}
    for n, batch in enumerate(BATCHES):
        for x in range(NX):
            for y in range(NY):
                for core in range(NCORE):
                    classes = {c: [] for c in range(NCOL)}
                    for kind, unit in batch:
                        row = other_row(kind, unit, core, x, y)
                        for block in range(LOCAL * row, LOCAL * row + LOCAL):
                            classes[block % NCOL].append((block, kind))
                    filled[x, y, n, core] = {c: sorted(v) for c, v in classes.items()}
                assert filled[x, y, n, 0] == filled[x, y, n, 1]
        sizes.append(max(len(v) for k, f in filled.items() if k[2] == n for v in f.values()))
    rows = []
    for x in range(NX):
        for y in range(NY):
            for col in range(NCOL):
                values = [x * NY + y, col]
                for n, batch in enumerate(BATCHES):
                    classes = filled[x, y, n, col % 2]
                    for kind, unit in batch:
                        row = other_row(kind, unit, col % 2, x, y)
                        for block in range(LOCAL * row, LOCAL * row + LOCAL):
                            target = block % NCOL
                            values.append(target * sizes[n] + classes[target].index((block, kind)))
                for n in range(len(BATCHES)):
                    held = filled[x, y, n, col % 2][col]
                    for slot in range(sizes[n]):
                        if slot < len(held):
                            values += [held[slot][0] // NCOL, int(held[slot][1] == "V")]
                        else:
                            values += [0, 2]
                rows.append(values)
    return tuple(sizes), np.asarray(rows, np.int32)


T_PIECES = 2
T_SLOTS = T_PIECES + LOCAL * len(ENTRIES)


def masked(x, start, end):
    orbital = lax.broadcasted_iota(jnp.int32, x.shape, 2)
    inside = (orbital >= start) & (orbital < end)
    return jnp.where(inside, x.astype(jnp.float32), 0.0).astype(jnp.bfloat16)


def in_vmem(value):
    return pltpu.with_memory_space_constraint(value, pltpu.VMEM)


def in_hbm(value):
    return pltpu.with_memory_space_constraint(value, pltpu.HBM)


VMEM_SPEC = pl.BlockSpec(memory_space=pltpu.VMEM)
HBM_SPEC = pl.BlockSpec(memory_space=pltpu.HBM)
SMEM_SPEC = pl.BlockSpec(memory_space=pltpu.SMEM)
MARK = jax.ShapeDtypeStruct((8, 128), jnp.float32)


def part_kernel(start, end, x_ref, out_ref, raw, sems):
    row, col = lax.axis_index("row"), lax.axis_index("col")

    def fetch(j):
        return pltpu.make_async_copy(x_ref.at[pl.ds(j * BLK + col * PIECE, PIECE)], raw.at[j], sems.at[j])

    for j in range(LOCAL):
        fetch(j).start()
    for j in range(LOCAL):
        fetch(j).wait()
        block = LOCAL * row + j
        values = masked(raw[j], start[block], end[block])
        out_ref[j * PIECE : (j + 1) * PIECE, :] = values.reshape(PIECE, WIDTH)


def own_part(start, end, coefficients):
    return pl.pallas_call(
        part_kernel,
        in_specs=[SMEM_SPEC] * 2 + [HBM_SPEC],
        out_specs=VMEM_SPEC,
        out_shape=pltpu.VMEM((PART, WIDTH), jnp.bfloat16),
        scratch_shapes=[pltpu.VMEM((LOCAL, PIECE, NAUX, OCC), jnp.bfloat16), pltpu.SemaphoreType.DMA((LOCAL,))],
        compiler_params=pltpu.CompilerParams(vmem_limit_bytes=6 << 20),
        cost_estimate=pl.CostEstimate(flops=0, bytes_accessed=5 << 19, transcendentals=0),
        name="own_part",
    )(start, end, in_hbm(coefficients))


CHUNK = 64


def rows_kernel(tab, start, end, x_ref, out_ref, mark_ref, raw, sems):
    steps = ROWS // CHUNK
    mark_ref[...] = jnp.zeros_like(mark_ref)

    def fetch(n):
        return pltpu.make_async_copy(x_ref.at[pl.ds(n * CHUNK, CHUNK)], raw.at[lax.rem(n, 4)], sems.at[lax.rem(n, 4)])

    for n in range(3):
        fetch(n).start()

    def step(n, carry):
        @pl.when(n + 3 < steps)
        def _():
            fetch(n + 3).start()

        fetch(n).wait()
        block = LOCAL * tab[0] + lax.div(n, BLK // CHUNK)
        values = masked(raw[lax.rem(n, 4)], start[block], end[block]).reshape(CHUNK, WIDTH)
        at = pl.ds(pl.multiple_of(n * CHUNK, CHUNK), CHUNK)
        for s in range(NSL):
            out_ref[s, at, :] = values[:, s * SLW : (s + 1) * SLW]
        return carry

    lax.fori_loop(0, steps, step, 0)


def own_rows(scalars, coefficients):
    return pl.pallas_call(
        rows_kernel,
        in_specs=[SMEM_SPEC] * 3 + [HBM_SPEC],
        out_specs=[VMEM_SPEC] * 2,
        out_shape=[pltpu.VMEM((NSL, ROWS, SLW), jnp.bfloat16), MARK],
        scratch_shapes=[pltpu.VMEM((4, CHUNK, NAUX, OCC), jnp.bfloat16), pltpu.SemaphoreType.DMA((4,))],
        compiler_params=pltpu.CompilerParams(vmem_limit_bytes=12 << 20),
        cost_estimate=pl.CostEstimate(flops=0, bytes_accessed=20 << 20, transcendentals=0),
        name="own_rows",
    )(*scalars, in_hbm(coefficients))


def product_kernel(n, *refs):
    parts, rows, outs, mark_ref, acc = refs[:n], refs[n], refs[n + 2 : 2 * n + 2], refs[2 * n + 2], refs[2 * n + 3]
    mark_ref[...] = jnp.zeros_like(mark_ref)
    for s in range(NSL):
        left = jnp.concatenate([part[:, s * SLW : (s + 1) * SLW] for part in parts], axis=0)
        term = lax.dot_general(left, rows[s], (((1,), (1,)), ((), ())), preferred_element_type=jnp.float32)
        if s == 0:
            acc[...] = term
        else:
            acc[...] += term
    for i, out in enumerate(outs):
        out[...] = acc[i * PART : (i + 1) * PART, :]


def products(parts, rows, token):
    n = len(parts)
    return pl.pallas_call(
        functools.partial(product_kernel, n),
        in_specs=[VMEM_SPEC] * (n + 1) + [pl.BlockSpec(memory_space=pl.ANY)],
        out_specs=[VMEM_SPEC] * (n + 1),
        out_shape=[pltpu.VMEM((PART, ROWS), jnp.float32)] * n + [MARK],
        scratch_shapes=[pltpu.VMEM((n * PART, ROWS), jnp.float32)],
        compiler_params=pltpu.CompilerParams(vmem_limit_bytes=12 << 20),
        cost_estimate=pl.CostEstimate(
            flops=2 * n * PART * ROWS * WIDTH, bytes_accessed=(10 << 20) + n * (3 << 19), transcendentals=0
        ),
        name="products",
    )(*[in_vmem(part) for part in parts], in_vmem(rows), token)


def stream_kernel(n, *refs):
    parts, rows, outs = refs[:n], refs[n], refs[n + 2 : 2 * n + 2]
    mark_ref, left, right, acc, left_sem, right_sem = refs[2 * n + 2 :]
    mark_ref[...] = jnp.zeros_like(mark_ref)

    def copies(s):
        span = pl.ds(s * SLW, SLW)
        found = [pltpu.make_async_copy(rows.at[s], right.at[s], right_sem.at[s])]
        for i, part in enumerate(parts):
            target = left.at[s, pl.ds(i * PART, PART), :]
            found.append(pltpu.make_async_copy(part.at[:, span], target, left_sem.at[i, s]))
        return found

    for s in range(NSL):
        for copy in copies(s):
            copy.start()
    for s in range(NSL):
        for copy in copies(s):
            copy.wait()
        term = lax.dot_general(left[s], right[s], (((1,), (1,)), ((), ())), preferred_element_type=jnp.float32)
        if s == 0:
            acc[...] = term
        else:
            acc[...] += term
    for i, out in enumerate(outs):
        out[...] = acc[i * PART : (i + 1) * PART, :]


def stream_products(parts, rows, token):
    n = len(parts)
    return pl.pallas_call(
        functools.partial(stream_kernel, n),
        in_specs=[HBM_SPEC] * (n + 1) + [pl.BlockSpec(memory_space=pl.ANY)],
        out_specs=[VMEM_SPEC] * (n + 1),
        out_shape=[pltpu.VMEM((PART, ROWS), jnp.float32)] * n + [MARK],
        scratch_shapes=[
            pltpu.VMEM((NSL, n * PART, SLW), jnp.bfloat16),
            pltpu.VMEM((NSL, ROWS, SLW), jnp.bfloat16),
            pltpu.VMEM((n * PART, ROWS), jnp.float32),
            pltpu.SemaphoreType.DMA((n, NSL)),
            pltpu.SemaphoreType.DMA((NSL,)),
        ],
        compiler_params=pltpu.CompilerParams(vmem_limit_bytes=20 << 20),
        cost_estimate=pl.CostEstimate(
            flops=2 * n * PART * ROWS * WIDTH, bytes_accessed=(10 << 20) + n * (3 << 19), transcendentals=0
        ),
        name="stream_products",
    )(*[in_hbm(part) for part in parts], in_hbm(rows), token)


def touch_kernel(rows_ref, token_ref, mark_ref):
    mark_ref[...] = jnp.zeros_like(mark_ref)


def touch(rows, token):
    return pl.pallas_call(
        touch_kernel,
        in_specs=[VMEM_SPEC, pl.BlockSpec(memory_space=pl.ANY)],
        out_specs=VMEM_SPEC,
        out_shape=MARK,
        compiler_params=pltpu.CompilerParams(vmem_limit_bytes=1 << 20),
        cost_estimate=pl.CostEstimate(flops=0, bytes_accessed=1 << 12, transcendentals=0),
        name="touch",
    )(in_vmem(rows), token)


def pack_kernel(first, batch, tab, *refs):
    *parts, _, out_ref, mark_ref, made, sem = refs
    mark_ref[...] = jnp.zeros_like(mark_ref)
    for n, (kind, _) in enumerate(batch):
        part = parts[n]
        for j in range(LOCAL):
            where = tab[T_PIECES + LOCAL * (first + n) + j]
            if kind == "V":
                made[where] = part[:, j * BLK : (j + 1) * BLK]
                continue
            for k in range(LOCAL):
                piece = part[j * PIECE : (j + 1) * PIECE, k * BLK : (k + 1) * BLK]
                made[where, k * PIECE : (k + 1) * PIECE, :] = piece
    copy = pltpu.make_async_copy(made, out_ref, sem)
    copy.start()
    copy.wait()


def pack(tab, first, batch, size, parts, token):
    return pl.pallas_call(
        functools.partial(pack_kernel, first, batch),
        in_specs=[SMEM_SPEC] + [VMEM_SPEC] * len(parts) + [pl.BlockSpec(memory_space=pl.ANY)],
        out_specs=[HBM_SPEC, VMEM_SPEC],
        out_shape=[pltpu.HBM((NCOL * size, PART, BLK), jnp.float32), MARK],
        scratch_shapes=[pltpu.VMEM((NCOL * size, PART, BLK), jnp.float32), pltpu.SemaphoreType.DMA],
        compiler_params=pltpu.CompilerParams(vmem_limit_bytes=6 << 20),
        cost_estimate=pl.CostEstimate(flops=0, bytes_accessed=3 << 20, transcendentals=0),
        name="pack",
    )(tab, *[in_vmem(part) for part in parts], token)


def place_tiles(tab, flags, number, sizes, ref, made, k):
    size = sizes[number]
    for n in range(size):
        at = T_SLOTS + 2 * (sum(sizes[:number]) + n)
        slot, kind = tab[at], tab[at + 1]
        weight = flags[SLOTS * k + slot].astype(jnp.float32)

        def tile(n=n, weight=weight):
            found = [ref[c * size + n, k * PIECE : (k + 1) * PIECE, :] for c in range(NCOL)]
            return jnp.concatenate(found, axis=0) * weight

        @pl.when(kind == 0)
        def _(slot=slot, tile=tile):
            made[k, pl.ds(slot, BLK, stride=SLOTS), :] = tile().T

        @pl.when(kind == 1)
        def _(slot=slot, tile=tile):
            made[k, pl.ds(slot, BLK, stride=SLOTS), :] = tile()


def early_kernel(sizes, tab, flags, *refs):
    count = len(refs) // 2 - 1
    given, made, pieces, sems = refs[:count], refs[count], refs[count + 1 : -1], refs[-1]
    copies = [pltpu.make_async_copy(ref, piece, sems.at[n]) for n, (ref, piece) in enumerate(zip(given, pieces))]
    for copy in copies:
        copy.start()
    for copy in copies:
        copy.wait()
    for k in range(LOCAL):
        for number, ref in enumerate(pieces):
            place_tiles(tab, flags, number, sizes, ref, made, k)


def place_early(tab, flags, sizes, pieces):
    return pl.pallas_call(
        functools.partial(early_kernel, sizes),
        in_specs=[SMEM_SPEC] * 2 + [HBM_SPEC] * len(pieces),
        out_specs=VMEM_SPEC,
        out_shape=pltpu.VMEM((LOCAL, BLK * SLOTS, BLK), jnp.float32),
        scratch_shapes=[pltpu.VMEM(piece.shape, jnp.float32) for piece in pieces]
        + [pltpu.SemaphoreType.DMA((len(pieces),))],
        compiler_params=pltpu.CompilerParams(vmem_limit_bytes=10 << 20),
        cost_estimate=pl.CostEstimate(flops=0, bytes_accessed=6 << 20, transcendentals=0),
        name="place_early",
    )(tab, flags, *[in_hbm(piece) for piece in pieces])


def late_kernel(sizes, tab, flags, early, piece, out_ref, made, sems, early_sem):
    def send(k):
        return pltpu.make_async_copy(made.at[k], out_ref.at[pl.ds(k * BLK * SLOTS, BLK * SLOTS), :], sems.at[k])

    copy = pltpu.make_async_copy(early, made, early_sem)
    copy.start()
    copy.wait()
    for k in range(LOCAL):
        place_tiles(tab, flags, len(sizes) - 1, sizes, piece, made, k)
        send(k).start()
    for k in range(LOCAL):
        send(k).wait()


def place_late(tab, flags, sizes, early, piece):
    return pl.pallas_call(
        functools.partial(late_kernel, sizes),
        in_specs=[SMEM_SPEC] * 2 + [VMEM_SPEC] * 2,
        out_specs=HBM_SPEC,
        out_shape=jax.ShapeDtypeStruct((ROWS * SLOTS, BLK), jnp.float32),
        scratch_shapes=[
            pltpu.VMEM((LOCAL, BLK * SLOTS, BLK), jnp.float32),
            pltpu.SemaphoreType.DMA((LOCAL,)),
            pltpu.SemaphoreType.DMA,
        ],
        compiler_params=pltpu.CompilerParams(vmem_limit_bytes=8 << 20),
        cost_estimate=pl.CostEstimate(flops=0, bytes_accessed=7 << 20, transcendentals=0),
        name="place_late",
    )(tab, flags, in_vmem(early), in_vmem(piece))


def flags_kernel(tab, pairs_ref, out_ref):
    first = jnp.minimum(pairs_ref[0:1, :], pairs_ref[1:2, :])
    second = jnp.maximum(pairs_ref[0:1, :], pairs_ref[1:2, :])
    codes = first * 256 + second
    for i in range(LOCAL):
        a = LOCAL * tab[0] + i
        for slot in range(SLOTS):
            b = tab[1] + NCOL * slot
            wanted = jnp.minimum(a, b) * 256 + jnp.maximum(a, b)
            out_ref[SLOTS * i + slot] = jnp.max((codes == wanted).astype(jnp.int32))


def listed_flags(tab, pair_list):
    return pl.pallas_call(
        flags_kernel,
        in_specs=[SMEM_SPEC, VMEM_SPEC],
        out_specs=SMEM_SPEC,
        out_shape=jax.ShapeDtypeStruct((LOCAL * SLOTS,), jnp.int32),
        compiler_params=pltpu.CompilerParams(vmem_limit_bytes=1 << 20),
        cost_estimate=pl.CostEstimate(flops=1 << 20, bytes_accessed=1 << 14, transcendentals=0),
        name="listed_flags",
    )(tab, pair_list.T)


def choose_kernel(tab, even_ref, odd_ref, out_ref, sem):
    core = lax.rem(tab[1], NCORE)
    for which, ref in enumerate((even_ref, odd_ref)):

        @pl.when(core == which)
        def _(ref=ref):
            pltpu.make_async_copy(ref, out_ref, sem).start()

    pltpu.make_async_copy(even_ref, out_ref, sem).wait()


def choose(tab, even, odd, late):
    return pl.pallas_call(
        choose_kernel,
        in_specs=[SMEM_SPEC] + [pl.BlockSpec(memory_space=pl.ANY)] * 2,
        out_specs=VMEM_SPEC,
        out_shape=pltpu.VMEM((PART, WIDTH), jnp.bfloat16),
        scratch_shapes=[pltpu.SemaphoreType.DMA],
        compiler_params=pltpu.CompilerParams(vmem_limit_bytes=4 << 20),
        cost_estimate=pl.CostEstimate(flops=0, bytes_accessed=5 << 19, transcendentals=0),
        name="choose",
    )(tab, in_hbm(even) if late else even, in_hbm(odd) if late else odd)


def per_device(coefficients, range_start, range_end, pair_list):
    sizes, table = tables()
    row, col = lax.axis_index("row"), lax.axis_index("col")
    tab = lax.dynamic_index_in_dim(jnp.asarray(table), row * NCOL + col, 0, keepdims=False)
    scalars = (in_hbm(tab), in_hbm(range_start), in_hbm(range_end))
    held = {0: own_part(*scalars[1:], coefficients)}
    rows, token = own_rows(scalars, coefficients)
    flags = listed_flags(tab, pair_list)
    made = {}

    def send(unit):
        a, b = UNITS[unit][2]
        source = held[a] if a == b else choose(tab, held[a], held[b], unit > 8)
        held[unit] = lax.ppermute(source, AXES, shifted(step_to(unit)))

    def multiply(group, token, how=products):
        *results, token = how([held[u] for u in group], rows, token)
        for unit, product in zip(group, results):
            made["U", unit] = product
        return token

    def send_back(unit):
        made["V", unit] = lax.ppermute(made["U", unit], AXES, shifted(step_back(unit)))

    def gate(units, token, back=()):
        found = [held[u] for u in units] + [made["V", u] for u in back]
        *values, token = lax.optimization_barrier((*found, token))
        held.update(zip(units, values))
        made.update({("V", u): value for u, value in zip(back, values[len(units) :])})
        return token

    for unit in (1, 2, 3, 4):
        send(unit)
    token = gate((1, 2, 3, 4), token)
    for unit in (5, 6, 7):
        send(unit)
    token = multiply(GROUPS[0], token)
    token = gate((5,), token)
    send(8)
    send(9)

    def ship(number, token):
        first = sum(len(earlier) for earlier in BATCHES[:number])
        batch = BATCHES[number]
        message, token = pack(tab, first, batch, sizes[number], [made[entry] for entry in batch], token)
        return lax.all_to_all(message, "col", 0, 0, tiled=True), token

    token = multiply(GROUPS[1], token)
    send_back(5)
    token = multiply(GROUPS[2], token)
    piece_a, token = ship(0, token)
    token = gate((8, 9), token)
    send(11)
    send(10)
    token = multiply(GROUPS[3], token, stream_products)
    send_back(8)
    send_back(9)
    made["U", 7], token = lax.optimization_barrier((made["U", 7], token))
    send_back(7)
    token = touch(rows, token)
    token = multiply(GROUPS[4], token)
    piece_b, token = ship(1, token)
    early = place_early(tab, flags, sizes, [piece_a])
    return place_late(tab, flags, sizes, early, piece_b).reshape(ROWS, SLOTS, 1, BLK)


def solution(mesh):
    in_specs = (P("row", None, None), P(), P(), P())
    out_specs = P("row", None, "col", None)
    return jax.shard_map(per_device, mesh=mesh, in_specs=in_specs, out_specs=out_specs, check_vma=False)
```

```python
import functools

import jax
import jax.numpy as jnp
import numpy as np
from jax import lax
from jax.experimental import pallas as pl
from jax.experimental.pallas import tpu as pltpu
from jax.sharding import PartitionSpec as P

BLK = 128
NX, NY, NZ, NCORE = 4, 4, 4, 2
NCOL = NZ * NCORE
NDEV = NX * NY * NCOL
LOCAL = 5
ROWS = LOCAL * BLK
NAUX, OCC = 32, 256
WIDTH = NAUX * OCC
PIECE = BLK // NCOL
PART = LOCAL * PIECE
NSL = 8
SLW = WIDTH // NSL
SLOTS = LOCAL * NX * NY // NCOL
AXES = ("row", "col")

UNITS = (
    ((0, 0), (0, 0), None),
    ((0, 1), (1, 0), (0, 0)),
    ((1, 0), (0, 1), (0, 0)),
    ((3, 0), (3, 0), (0, 0)),
    ((0, 3), (0, 3), (0, 0)),
    ((1, 1), (1, 1), (1, 1)),
    ((2, 0), (2, 0), (3, 3)),
    ((1, 3), (1, 3), (2, 1)),
    ((2, 1), (2, 1), (5, 5)),
    ((1, 2), (1, 2), (5, 5)),
    ((0, 2), (2, 2), (4, 8)),
    ((2, 2), (0, 2), (9, 9)),
)
BACK = (5, 7, 8, 9)
GROUPS = ((0, 1, 2, 3, 4), (5,), (6, 7), (8, 9), (10, 11))
BATCHES = (
    (("U", 0), ("U", 1), ("U", 2), ("U", 3), ("U", 4), ("U", 5), ("V", 5), ("U", 6), ("U", 7)),
    (("V", 7), ("U", 8), ("U", 9), ("U", 10), ("U", 11), ("V", 8), ("V", 9)),
)
ENTRIES = tuple(entry for batch in BATCHES for entry in batch)


def dev(x, y, col):
    return (x * NY + y) * NCOL + col


def shifted(moves):
    return [
        (dev(x, y, col), dev((x + moves[col % 2][0]) % NX, (y + moves[col % 2][1]) % NY, col))
        for x in range(NX)
        for y in range(NY)
        for col in range(NCOL)
    ]


def step_to(unit):
    moves = []
    for core in range(NCORE):
        here, there = UNITS[unit][core], UNITS[UNITS[unit][2][core]][core]
        moves.append(((here[0] - there[0]) % NX, (here[1] - there[1]) % NY))
    return moves


def step_back(unit):
    return [(-UNITS[unit][core][0] % NX, -UNITS[unit][core][1] % NY) for core in range(NCORE)]


def other_row(kind, unit, core, x, y):
    m = UNITS[unit][core]
    sign = -1 if kind == "U" else 1
    return (x + sign * m[0]) % NX * NY + (y + sign * m[1]) % NY


@functools.cache
def tables():
    sizes = []
    filled = {}
    for n, batch in enumerate(BATCHES):
        for x in range(NX):
            for y in range(NY):
                for core in range(NCORE):
                    classes = {c: [] for c in range(NCOL)}
                    for kind, unit in batch:
                        row = other_row(kind, unit, core, x, y)
                        for block in range(LOCAL * row, LOCAL * row + LOCAL):
                            classes[block % NCOL].append((block, kind))
                    filled[x, y, n, core] = {c: sorted(v) for c, v in classes.items()}
                assert filled[x, y, n, 0] == filled[x, y, n, 1]
        sizes.append(max(len(v) for k, f in filled.items() if k[2] == n for v in f.values()))
    rows = []
    for x in range(NX):
        for y in range(NY):
            for col in range(NCOL):
                values = [x * NY + y, col]
                for n, batch in enumerate(BATCHES):
                    classes = filled[x, y, n, col % 2]
                    for kind, unit in batch:
                        row = other_row(kind, unit, col % 2, x, y)
                        for block in range(LOCAL * row, LOCAL * row + LOCAL):
                            target = block % NCOL
                            values.append(target * sizes[n] + classes[target].index((block, kind)))
                for n in range(len(BATCHES)):
                    held = filled[x, y, n, col % 2][col]
                    for slot in range(sizes[n]):
                        if slot < len(held):
                            values += [held[slot][0] // NCOL, int(held[slot][1] == "V")]
                        else:
                            values += [0, 2]
                rows.append(values)
    return tuple(sizes), np.asarray(rows, np.int32)


T_PIECES = 2
T_SLOTS = T_PIECES + LOCAL * len(ENTRIES)


def masked(x, start, end):
    orbital = lax.broadcasted_iota(jnp.int32, x.shape, 2)
    inside = (orbital >= start) & (orbital < end)
    return jnp.where(inside, x.astype(jnp.float32), 0.0).astype(jnp.bfloat16)


def in_vmem(value):
    return pltpu.with_memory_space_constraint(value, pltpu.VMEM)


def in_hbm(value):
    return pltpu.with_memory_space_constraint(value, pltpu.HBM)


VMEM_SPEC = pl.BlockSpec(memory_space=pltpu.VMEM)
HBM_SPEC = pl.BlockSpec(memory_space=pltpu.HBM)
SMEM_SPEC = pl.BlockSpec(memory_space=pltpu.SMEM)
MARK = jax.ShapeDtypeStruct((8, 128), jnp.float32)


def part_kernel(start, end, x_ref, out_ref, raw, sems):
    row, col = lax.axis_index("row"), lax.axis_index("col")

    def fetch(j):
        return pltpu.make_async_copy(x_ref.at[pl.ds(j * BLK + col * PIECE, PIECE)], raw.at[j], sems.at[j])

    for j in range(LOCAL):
        fetch(j).start()
    for j in range(LOCAL):
        fetch(j).wait()
        block = LOCAL * row + j
        values = masked(raw[j], start[block], end[block])
        out_ref[j * PIECE : (j + 1) * PIECE, :] = values.reshape(PIECE, WIDTH)


def own_part(start, end, coefficients):
    return pl.pallas_call(
        part_kernel,
        in_specs=[SMEM_SPEC] * 2 + [HBM_SPEC],
        out_specs=VMEM_SPEC,
        out_shape=pltpu.VMEM((PART, WIDTH), jnp.bfloat16),
        scratch_shapes=[pltpu.VMEM((LOCAL, PIECE, NAUX, OCC), jnp.bfloat16), pltpu.SemaphoreType.DMA((LOCAL,))],
        compiler_params=pltpu.CompilerParams(vmem_limit_bytes=6 << 20),
        cost_estimate=pl.CostEstimate(flops=0, bytes_accessed=5 << 19, transcendentals=0),
        name="own_part",
    )(start, end, in_hbm(coefficients))


CHUNK = 64


def rows_kernel(tab, start, end, x_ref, out_ref, mark_ref, raw, sems):
    steps = ROWS // CHUNK
    mark_ref[...] = jnp.zeros_like(mark_ref)

    def fetch(n):
        return pltpu.make_async_copy(x_ref.at[pl.ds(n * CHUNK, CHUNK)], raw.at[lax.rem(n, 4)], sems.at[lax.rem(n, 4)])

    for n in range(3):
        fetch(n).start()

    def step(n, carry):
        @pl.when(n + 3 < steps)
        def _():
            fetch(n + 3).start()

        fetch(n).wait()
        block = LOCAL * tab[0] + lax.div(n, BLK // CHUNK)
        values = masked(raw[lax.rem(n, 4)], start[block], end[block]).reshape(CHUNK, WIDTH)
        at = pl.ds(pl.multiple_of(n * CHUNK, CHUNK), CHUNK)
        for s in range(NSL):
            out_ref[s, at, :] = values[:, s * SLW : (s + 1) * SLW]
        return carry

    lax.fori_loop(0, steps, step, 0)


def own_rows(scalars, coefficients):
    return pl.pallas_call(
        rows_kernel,
        in_specs=[SMEM_SPEC] * 3 + [HBM_SPEC],
        out_specs=[VMEM_SPEC] * 2,
        out_shape=[pltpu.VMEM((NSL, ROWS, SLW), jnp.bfloat16), MARK],
        scratch_shapes=[pltpu.VMEM((4, CHUNK, NAUX, OCC), jnp.bfloat16), pltpu.SemaphoreType.DMA((4,))],
        compiler_params=pltpu.CompilerParams(vmem_limit_bytes=12 << 20),
        cost_estimate=pl.CostEstimate(flops=0, bytes_accessed=20 << 20, transcendentals=0),
        name="own_rows",
    )(*scalars, in_hbm(coefficients))


def product_kernel(widths, *refs):
    n, m = len(widths), sum(widths)
    given, rows, outs, mark_ref, acc = refs[:m], refs[m], refs[m + 2 : m + n + 2], refs[m + n + 2], refs[m + n + 3]
    parts = [given[sum(widths[:i]) : sum(widths[: i + 1])] for i in range(n)]
    mark_ref[...] = jnp.zeros_like(mark_ref)
    for s in range(NSL):
        span = slice(s * SLW, (s + 1) * SLW)
        left = jnp.concatenate([sum([ref[:, span] for ref in part[1:]], part[0][:, span]) for part in parts], axis=0)
        term = lax.dot_general(left, rows[s], (((1,), (1,)), ((), ())), preferred_element_type=jnp.float32)
        if s == 0:
            acc[...] = term
        else:
            acc[...] += term
    for i, out in enumerate(outs):
        out[...] = acc[i * PART : (i + 1) * PART, :]


def products(parts, rows, token):
    parts = [part if isinstance(part, tuple) else (part,) for part in parts]
    widths = [len(part) for part in parts]
    n, given = len(parts), [array for part in parts for array in part]
    return pl.pallas_call(
        functools.partial(product_kernel, widths),
        in_specs=[VMEM_SPEC] * (len(given) + 1) + [pl.BlockSpec(memory_space=pl.ANY)],
        out_specs=[VMEM_SPEC] * (n + 1),
        out_shape=[pltpu.VMEM((PART, ROWS), jnp.float32)] * n + [MARK],
        scratch_shapes=[pltpu.VMEM((n * PART, ROWS), jnp.float32)],
        compiler_params=pltpu.CompilerParams(vmem_limit_bytes=12 << 20),
        cost_estimate=pl.CostEstimate(
            flops=2 * n * PART * ROWS * WIDTH, bytes_accessed=(10 << 20) + n * (3 << 19), transcendentals=0
        ),
        name="products",
    )(*[in_vmem(array) for array in given], in_vmem(rows), token)


def stream_kernel(n, *refs):
    parts, rows, outs = refs[:n], refs[n], refs[n + 2 : 2 * n + 2]
    mark_ref, left, right, acc, left_sem, right_sem = refs[2 * n + 2 :]
    mark_ref[...] = jnp.zeros_like(mark_ref)

    def copies(s):
        span = pl.ds(s * SLW, SLW)
        found = [pltpu.make_async_copy(rows.at[s], right.at[s], right_sem.at[s])]
        for i, part in enumerate(parts):
            target = left.at[s, pl.ds(i * PART, PART), :]
            found.append(pltpu.make_async_copy(part.at[:, span], target, left_sem.at[i, s]))
        return found

    for s in range(NSL):
        for copy in copies(s):
            copy.start()
    for s in range(NSL):
        for copy in copies(s):
            copy.wait()
        term = lax.dot_general(left[s], right[s], (((1,), (1,)), ((), ())), preferred_element_type=jnp.float32)
        if s == 0:
            acc[...] = term
        else:
            acc[...] += term
    for i, out in enumerate(outs):
        out[...] = acc[i * PART : (i + 1) * PART, :]


def stream_products(parts, rows, token):
    n = len(parts)
    return pl.pallas_call(
        functools.partial(stream_kernel, n),
        in_specs=[HBM_SPEC] * (n + 1) + [pl.BlockSpec(memory_space=pl.ANY)],
        out_specs=[VMEM_SPEC] * (n + 1),
        out_shape=[pltpu.VMEM((PART, ROWS), jnp.float32)] * n + [MARK],
        scratch_shapes=[
            pltpu.VMEM((NSL, n * PART, SLW), jnp.bfloat16),
            pltpu.VMEM((NSL, ROWS, SLW), jnp.bfloat16),
            pltpu.VMEM((n * PART, ROWS), jnp.float32),
            pltpu.SemaphoreType.DMA((n, NSL)),
            pltpu.SemaphoreType.DMA((NSL,)),
        ],
        compiler_params=pltpu.CompilerParams(vmem_limit_bytes=20 << 20),
        cost_estimate=pl.CostEstimate(
            flops=2 * n * PART * ROWS * WIDTH, bytes_accessed=(10 << 20) + n * (3 << 19), transcendentals=0
        ),
        name="stream_products",
    )(*[in_hbm(part) for part in parts], in_hbm(rows), token)


def touch_kernel(rows_ref, token_ref, mark_ref):
    mark_ref[...] = jnp.zeros_like(mark_ref)


def touch(rows, token):
    return pl.pallas_call(
        touch_kernel,
        in_specs=[VMEM_SPEC, pl.BlockSpec(memory_space=pl.ANY)],
        out_specs=VMEM_SPEC,
        out_shape=MARK,
        compiler_params=pltpu.CompilerParams(vmem_limit_bytes=1 << 20),
        cost_estimate=pl.CostEstimate(flops=0, bytes_accessed=1 << 12, transcendentals=0),
        name="touch",
    )(in_vmem(rows), token)


def pack_kernel(first, batch, tab, *refs):
    *parts, _, out_ref, mark_ref, made, sem = refs
    mark_ref[...] = jnp.zeros_like(mark_ref)
    for n, (kind, _) in enumerate(batch):
        part = parts[n]
        for j in range(LOCAL):
            where = tab[T_PIECES + LOCAL * (first + n) + j]
            if kind == "V":
                made[where] = part[:, j * BLK : (j + 1) * BLK]
                continue
            for k in range(LOCAL):
                piece = part[j * PIECE : (j + 1) * PIECE, k * BLK : (k + 1) * BLK]
                made[where, k * PIECE : (k + 1) * PIECE, :] = piece
    copy = pltpu.make_async_copy(made, out_ref, sem)
    copy.start()
    copy.wait()


def pack(tab, first, batch, size, parts, token):
    return pl.pallas_call(
        functools.partial(pack_kernel, first, batch),
        in_specs=[SMEM_SPEC] + [VMEM_SPEC] * len(parts) + [pl.BlockSpec(memory_space=pl.ANY)],
        out_specs=[HBM_SPEC, VMEM_SPEC],
        out_shape=[pltpu.HBM((NCOL * size, PART, BLK), jnp.float32), MARK],
        scratch_shapes=[pltpu.VMEM((NCOL * size, PART, BLK), jnp.float32), pltpu.SemaphoreType.DMA],
        compiler_params=pltpu.CompilerParams(vmem_limit_bytes=6 << 20),
        cost_estimate=pl.CostEstimate(flops=0, bytes_accessed=3 << 20, transcendentals=0),
        name="pack",
    )(tab, *[in_vmem(part) for part in parts], token)


def place_tiles(tab, flags, number, sizes, ref, made, k):
    size = sizes[number]
    for n in range(size):
        at = T_SLOTS + 2 * (sum(sizes[:number]) + n)
        slot, kind = tab[at], tab[at + 1]
        weight = flags[SLOTS * k + slot].astype(jnp.float32)

        def tile(n=n, weight=weight):
            found = [ref[c * size + n, k * PIECE : (k + 1) * PIECE, :] for c in range(NCOL)]
            return jnp.concatenate(found, axis=0) * weight

        @pl.when(kind == 0)
        def _(slot=slot, tile=tile):
            made[k, pl.ds(slot, BLK, stride=SLOTS), :] = tile().T

        @pl.when(kind == 1)
        def _(slot=slot, tile=tile):
            made[k, pl.ds(slot, BLK, stride=SLOTS), :] = tile()


def early_kernel(sizes, tab, flags, *refs):
    count = len(refs) // 2 - 1
    given, made, pieces, sems = refs[:count], refs[count], refs[count + 1 : -1], refs[-1]
    copies = [pltpu.make_async_copy(ref, piece, sems.at[n]) for n, (ref, piece) in enumerate(zip(given, pieces))]
    for copy in copies:
        copy.start()
    for copy in copies:
        copy.wait()
    for k in range(LOCAL):
        for number, ref in enumerate(pieces):
            place_tiles(tab, flags, number, sizes, ref, made, k)


def place_early(tab, flags, sizes, pieces):
    return pl.pallas_call(
        functools.partial(early_kernel, sizes),
        in_specs=[SMEM_SPEC] * 2 + [HBM_SPEC] * len(pieces),
        out_specs=VMEM_SPEC,
        out_shape=pltpu.VMEM((LOCAL, BLK * SLOTS, BLK), jnp.float32),
        scratch_shapes=[pltpu.VMEM(piece.shape, jnp.float32) for piece in pieces]
        + [pltpu.SemaphoreType.DMA((len(pieces),))],
        compiler_params=pltpu.CompilerParams(vmem_limit_bytes=10 << 20),
        cost_estimate=pl.CostEstimate(flops=0, bytes_accessed=6 << 20, transcendentals=0),
        name="place_early",
    )(tab, flags, *[in_hbm(piece) for piece in pieces])


def late_kernel(sizes, tab, flags, early, piece, out_ref, made, sems, early_sem):
    def send(k):
        return pltpu.make_async_copy(made.at[k], out_ref.at[pl.ds(k * BLK * SLOTS, BLK * SLOTS), :], sems.at[k])

    copy = pltpu.make_async_copy(early, made, early_sem)
    copy.start()
    copy.wait()
    for k in range(LOCAL):
        place_tiles(tab, flags, len(sizes) - 1, sizes, piece, made, k)
        send(k).start()
    for k in range(LOCAL):
        send(k).wait()


def place_late(tab, flags, sizes, early, piece):
    return pl.pallas_call(
        functools.partial(late_kernel, sizes),
        in_specs=[SMEM_SPEC] * 2 + [VMEM_SPEC] * 2,
        out_specs=HBM_SPEC,
        out_shape=jax.ShapeDtypeStruct((ROWS * SLOTS, BLK), jnp.float32),
        scratch_shapes=[
            pltpu.VMEM((LOCAL, BLK * SLOTS, BLK), jnp.float32),
            pltpu.SemaphoreType.DMA((LOCAL,)),
            pltpu.SemaphoreType.DMA,
        ],
        compiler_params=pltpu.CompilerParams(vmem_limit_bytes=8 << 20),
        cost_estimate=pl.CostEstimate(flops=0, bytes_accessed=7 << 20, transcendentals=0),
        name="place_late",
    )(tab, flags, in_vmem(early), in_vmem(piece))


def flags_kernel(tab, pairs_ref, out_ref):
    first = jnp.minimum(pairs_ref[0:1, :], pairs_ref[1:2, :])
    second = jnp.maximum(pairs_ref[0:1, :], pairs_ref[1:2, :])
    codes = first * 256 + second
    for i in range(LOCAL):
        a = LOCAL * tab[0] + i
        for slot in range(SLOTS):
            b = tab[1] + NCOL * slot
            wanted = jnp.minimum(a, b) * 256 + jnp.maximum(a, b)
            out_ref[SLOTS * i + slot] = jnp.max((codes == wanted).astype(jnp.int32))


def listed_flags(tab, pair_list):
    return pl.pallas_call(
        flags_kernel,
        in_specs=[SMEM_SPEC, VMEM_SPEC],
        out_specs=SMEM_SPEC,
        out_shape=jax.ShapeDtypeStruct((LOCAL * SLOTS,), jnp.int32),
        compiler_params=pltpu.CompilerParams(vmem_limit_bytes=1 << 20),
        cost_estimate=pl.CostEstimate(flops=1 << 20, bytes_accessed=1 << 14, transcendentals=0),
        name="listed_flags",
    )(tab, pair_list.T)


def choose_kernel(tab, even_ref, odd_ref, out_ref, sem):
    core = lax.rem(tab[1], NCORE)
    for which, ref in enumerate((even_ref, odd_ref)):

        @pl.when(core == which)
        def _(ref=ref):
            pltpu.make_async_copy(ref, out_ref, sem).start()

    pltpu.make_async_copy(even_ref, out_ref, sem).wait()


def choose(tab, even, odd, late):
    return pl.pallas_call(
        choose_kernel,
        in_specs=[SMEM_SPEC] + [pl.BlockSpec(memory_space=pl.ANY)] * 2,
        out_specs=VMEM_SPEC,
        out_shape=pltpu.VMEM((PART, WIDTH), jnp.bfloat16),
        scratch_shapes=[pltpu.SemaphoreType.DMA],
        compiler_params=pltpu.CompilerParams(vmem_limit_bytes=4 << 20),
        cost_estimate=pl.CostEstimate(flops=0, bytes_accessed=5 << 19, transcendentals=0),
        name="choose",
    )(tab, in_hbm(even) if late else even, in_hbm(odd) if late else odd)


def per_device(coefficients, range_start, range_end, pair_list):
    sizes, table = tables()
    row, col = lax.axis_index("row"), lax.axis_index("col")
    tab = lax.dynamic_index_in_dim(jnp.asarray(table), row * NCOL + col, 0, keepdims=False)
    scalars = (in_hbm(tab), in_hbm(range_start), in_hbm(range_end))
    held = {0: own_part(*scalars[1:], coefficients)}
    rows, token = own_rows(scalars, coefficients)
    flags = listed_flags(tab, pair_list)
    made = {}

    def send(unit):
        a, b = UNITS[unit][2]
        source = held[a] if a == b else choose(tab, held[a], held[b], unit > 8)
        held[unit] = lax.ppermute(source, AXES, shifted(step_to(unit)))

    def multiply(group, token, how=products):
        *results, token = how([held[u] for u in group], rows, token)
        for unit, product in zip(group, results):
            made["U", unit] = product
        return token

    def send_back(unit):
        made["V", unit] = lax.ppermute(made["U", unit], AXES, shifted(step_back(unit)))

    def gate(units, token, back=()):
        found = [held[u] for u in units] + [made["V", u] for u in back]
        *values, token = lax.optimization_barrier((*found, token))
        held.update(zip(units, values))
        made.update({("V", u): value for u, value in zip(back, values[len(units) :])})
        return token

    for unit in (1, 2, 3, 4):
        send(unit)
    token = gate((1, 2, 3, 4), token)
    for unit in (5, 6, 7):
        send(unit)
    token = multiply(GROUPS[0], token)
    token = gate((5,), token)
    send(8)
    send(9)

    def ship(number, token):
        first = sum(len(earlier) for earlier in BATCHES[:number])
        batch = BATCHES[number]
        message, token = pack(tab, first, batch, sizes[number], [made[entry] for entry in batch], token)
        return lax.all_to_all(message, "col", 0, 0, tiled=True), token

    token = multiply(GROUPS[1], token)
    send_back(5)
    token = multiply(GROUPS[2], token)
    piece_a, token = ship(0, token)
    token = gate((4, 8, 9), token)
    send(11)
    held[10] = tuple(lax.ppermute(held[u], AXES, shifted(step_to(10))[c::2]) for c, u in enumerate(UNITS[10][2]))
    token = multiply(GROUPS[3], token, stream_products)
    send_back(8)
    send_back(9)
    made["U", 7], token = lax.optimization_barrier((made["U", 7], token))
    send_back(7)
    token = touch(rows, token)
    token = multiply(GROUPS[4], token)
    piece_b, token = ship(1, token)
    early = place_early(tab, flags, sizes, [piece_a])
    return place_late(tab, flags, sizes, early, piece_b).reshape(ROWS, SLOTS, 1, BLK)


def solution(mesh):
    in_specs = (P("row", None, None), P(), P(), P())
    out_specs = P("row", None, "col", None)
    return jax.shard_map(per_device, mesh=mesh, in_specs=in_specs, out_specs=out_specs, check_vma=False)
```

```python
import functools

import jax
import jax.numpy as jnp
import numpy as np
from jax import lax
from jax.experimental import pallas as pl
from jax.experimental.pallas import tpu as pltpu
from jax.sharding import PartitionSpec as P

BLK = 128
NX, NY, NZ, NCORE = 4, 4, 4, 2
NCOL = NZ * NCORE
NDEV = NX * NY * NCOL
LOCAL = 5
ROWS = LOCAL * BLK
NAUX, OCC = 32, 256
WIDTH = NAUX * OCC
PIECE = BLK // NCOL
PART = LOCAL * PIECE
NSL = 8
SLW = WIDTH // NSL
SLOTS = LOCAL * NX * NY // NCOL
AXES = ("row", "col")

UNITS = (
    ((0, 0), (0, 0), None),
    ((0, 1), (1, 0), (0, 0)),
    ((1, 0), (0, 1), (0, 0)),
    ((3, 0), (3, 0), (0, 0)),
    ((0, 3), (0, 3), (0, 0)),
    ((1, 1), (1, 1), (1, 1)),
    ((2, 0), (2, 0), (3, 3)),
    ((1, 3), (1, 3), (2, 1)),
    ((2, 1), (2, 1), (5, 5)),
    ((1, 2), (1, 2), (5, 5)),
    ((0, 2), (2, 2), (4, 8)),
    ((2, 2), (0, 2), (9, 9)),
)
BACK = (5, 7, 8, 9)
GROUPS = ((0, 1, 2, 3, 4), (5,), (6, 7), (8, 9), (10, 11))
BATCHES = (
    (("U", 0), ("U", 1), ("U", 2), ("U", 3), ("U", 4), ("U", 5), ("V", 5), ("U", 6), ("U", 7)),
    (("V", 7), ("U", 8), ("U", 9), ("U", 10), ("U", 11), ("V", 8), ("V", 9)),
)
ENTRIES = tuple(entry for batch in BATCHES for entry in batch)


def dev(x, y, col):
    return (x * NY + y) * NCOL + col


def shifted(moves):
    return [
        (dev(x, y, col), dev((x + moves[col % 2][0]) % NX, (y + moves[col % 2][1]) % NY, col))
        for x in range(NX)
        for y in range(NY)
        for col in range(NCOL)
    ]


def step_to(unit):
    moves = []
    for core in range(NCORE):
        here, there = UNITS[unit][core], UNITS[UNITS[unit][2][core]][core]
        moves.append(((here[0] - there[0]) % NX, (here[1] - there[1]) % NY))
    return moves


def step_back(unit):
    return [(-UNITS[unit][core][0] % NX, -UNITS[unit][core][1] % NY) for core in range(NCORE)]


def other_row(kind, unit, core, x, y):
    m = UNITS[unit][core]
    sign = -1 if kind == "U" else 1
    return (x + sign * m[0]) % NX * NY + (y + sign * m[1]) % NY


@functools.cache
def tables():
    sizes = []
    filled = {}
    for n, batch in enumerate(BATCHES):
        for x in range(NX):
            for y in range(NY):
                for core in range(NCORE):
                    classes = {c: [] for c in range(NCOL)}
                    for kind, unit in batch:
                        row = other_row(kind, unit, core, x, y)
                        for block in range(LOCAL * row, LOCAL * row + LOCAL):
                            classes[block % NCOL].append((block, kind))
                    filled[x, y, n, core] = {c: sorted(v) for c, v in classes.items()}
                assert filled[x, y, n, 0] == filled[x, y, n, 1]
        sizes.append(max(len(v) for k, f in filled.items() if k[2] == n for v in f.values()))
    rows = []
    for x in range(NX):
        for y in range(NY):
            for col in range(NCOL):
                values = [x * NY + y, col]
                for n, batch in enumerate(BATCHES):
                    classes = filled[x, y, n, col % 2]
                    for kind, unit in batch:
                        row = other_row(kind, unit, col % 2, x, y)
                        for block in range(LOCAL * row, LOCAL * row + LOCAL):
                            target = block % NCOL
                            values.append(target * sizes[n] + classes[target].index((block, kind)))
                for n in range(len(BATCHES)):
                    held = filled[x, y, n, col % 2][col]
                    for slot in range(sizes[n]):
                        if slot < len(held):
                            values += [held[slot][0] // NCOL, int(held[slot][1] == "V")]
                        else:
                            values += [0, 2]
                rows.append(values)
    return tuple(sizes), np.asarray(rows, np.int32)


T_PIECES = 2
T_SLOTS = T_PIECES + LOCAL * len(ENTRIES)


def masked(x, start, end):
    orbital = lax.broadcasted_iota(jnp.int32, x.shape, 2)
    inside = (orbital >= start) & (orbital < end)
    return jnp.where(inside, x.astype(jnp.float32), 0.0).astype(jnp.bfloat16)


def in_vmem(value):
    return pltpu.with_memory_space_constraint(value, pltpu.VMEM)


def in_hbm(value):
    return pltpu.with_memory_space_constraint(value, pltpu.HBM)


VMEM_SPEC = pl.BlockSpec(memory_space=pltpu.VMEM)
HBM_SPEC = pl.BlockSpec(memory_space=pltpu.HBM)
SMEM_SPEC = pl.BlockSpec(memory_space=pltpu.SMEM)
MARK = jax.ShapeDtypeStruct((8, 128), jnp.float32)


def part_kernel(start, end, x_ref, out_ref, raw, sems):
    row, col = lax.axis_index("row"), lax.axis_index("col")

    def fetch(j):
        return pltpu.make_async_copy(x_ref.at[pl.ds(j * BLK + col * PIECE, PIECE)], raw.at[j], sems.at[j])

    for j in range(LOCAL):
        fetch(j).start()
    for j in range(LOCAL):
        fetch(j).wait()
        block = LOCAL * row + j
        values = masked(raw[j], start[block], end[block])
        out_ref[j * PIECE : (j + 1) * PIECE, :] = values.reshape(PIECE, WIDTH)


def own_part(start, end, coefficients):
    return pl.pallas_call(
        part_kernel,
        in_specs=[SMEM_SPEC] * 2 + [HBM_SPEC],
        out_specs=VMEM_SPEC,
        out_shape=pltpu.VMEM((PART, WIDTH), jnp.bfloat16),
        scratch_shapes=[pltpu.VMEM((LOCAL, PIECE, NAUX, OCC), jnp.bfloat16), pltpu.SemaphoreType.DMA((LOCAL,))],
        compiler_params=pltpu.CompilerParams(vmem_limit_bytes=6 << 20),
        cost_estimate=pl.CostEstimate(flops=0, bytes_accessed=5 << 19, transcendentals=0),
        name="own_part",
    )(start, end, in_hbm(coefficients))


CHUNK = 64


def rows_kernel(tab, start, end, x_ref, out_ref, mark_ref, raw, sems):
    steps = ROWS // CHUNK
    mark_ref[...] = jnp.zeros_like(mark_ref)

    def fetch(n):
        return pltpu.make_async_copy(x_ref.at[pl.ds(n * CHUNK, CHUNK)], raw.at[lax.rem(n, 4)], sems.at[lax.rem(n, 4)])

    for n in range(3):
        fetch(n).start()

    def step(n, carry):
        @pl.when(n + 3 < steps)
        def _():
            fetch(n + 3).start()

        fetch(n).wait()
        block = LOCAL * tab[0] + lax.div(n, BLK // CHUNK)
        values = masked(raw[lax.rem(n, 4)], start[block], end[block]).reshape(CHUNK, WIDTH)
        at = pl.ds(pl.multiple_of(n * CHUNK, CHUNK), CHUNK)
        for s in range(NSL):
            out_ref[s, at, :] = values[:, s * SLW : (s + 1) * SLW]
        return carry

    lax.fori_loop(0, steps, step, 0)


def own_rows(scalars, coefficients):
    return pl.pallas_call(
        rows_kernel,
        in_specs=[SMEM_SPEC] * 3 + [HBM_SPEC],
        out_specs=[VMEM_SPEC] * 2,
        out_shape=[pltpu.VMEM((NSL, ROWS, SLW), jnp.bfloat16), MARK],
        scratch_shapes=[pltpu.VMEM((4, CHUNK, NAUX, OCC), jnp.bfloat16), pltpu.SemaphoreType.DMA((4,))],
        compiler_params=pltpu.CompilerParams(vmem_limit_bytes=12 << 20),
        cost_estimate=pl.CostEstimate(flops=0, bytes_accessed=20 << 20, transcendentals=0),
        name="own_rows",
    )(*scalars, in_hbm(coefficients))


def product_kernel(widths, *refs):
    n, m = len(widths), sum(widths)
    given, rows, outs, mark_ref, acc = refs[:m], refs[m], refs[m + 2 : m + n + 2], refs[m + n + 2], refs[m + n + 3]
    parts = [given[sum(widths[:i]) : sum(widths[: i + 1])] for i in range(n)]
    mark_ref[...] = jnp.zeros_like(mark_ref)
    for s in range(NSL):
        span = slice(s * SLW, (s + 1) * SLW)
        left = jnp.concatenate([sum([ref[:, span] for ref in part[1:]], part[0][:, span]) for part in parts], axis=0)
        term = lax.dot_general(left, rows[s], (((1,), (1,)), ((), ())), preferred_element_type=jnp.float32)
        if s == 0:
            acc[...] = term
        else:
            acc[...] += term
    for i, out in enumerate(outs):
        out[...] = acc[i * PART : (i + 1) * PART, :]


def products(parts, rows, token):
    parts = [part if isinstance(part, tuple) else (part,) for part in parts]
    widths = [len(part) for part in parts]
    n, given = len(parts), [array for part in parts for array in part]
    return pl.pallas_call(
        functools.partial(product_kernel, widths),
        in_specs=[VMEM_SPEC] * (len(given) + 1) + [pl.BlockSpec(memory_space=pl.ANY)],
        out_specs=[VMEM_SPEC] * (n + 1),
        out_shape=[pltpu.VMEM((PART, ROWS), jnp.float32)] * n + [MARK],
        scratch_shapes=[pltpu.VMEM((n * PART, ROWS), jnp.float32)],
        compiler_params=pltpu.CompilerParams(vmem_limit_bytes=12 << 20),
        cost_estimate=pl.CostEstimate(
            flops=2 * n * PART * ROWS * WIDTH, bytes_accessed=(10 << 20) + n * (3 << 19), transcendentals=0
        ),
        name="products",
    )(*[in_vmem(array) for array in given], in_vmem(rows), token)


def stream_kernel(n, *refs):
    parts, rows, outs = refs[:n], refs[n], refs[n + 2 : 2 * n + 2]
    mark_ref, left, right, acc, left_sem, right_sem = refs[2 * n + 2 :]
    mark_ref[...] = jnp.zeros_like(mark_ref)

    def copies(s):
        span = pl.ds(s * SLW, SLW)
        found = [pltpu.make_async_copy(rows.at[s], right.at[s], right_sem.at[s])]
        for i, part in enumerate(parts):
            target = left.at[s, pl.ds(i * PART, PART), :]
            found.append(pltpu.make_async_copy(part.at[:, span], target, left_sem.at[i, s]))
        return found

    for s in range(NSL):
        for copy in copies(s):
            copy.start()
    for s in range(NSL):
        for copy in copies(s):
            copy.wait()
        term = lax.dot_general(left[s], right[s], (((1,), (1,)), ((), ())), preferred_element_type=jnp.float32)
        if s == 0:
            acc[...] = term
        else:
            acc[...] += term
    for i, out in enumerate(outs):
        out[...] = acc[i * PART : (i + 1) * PART, :]


def stream_products(parts, rows, token):
    n = len(parts)
    return pl.pallas_call(
        functools.partial(stream_kernel, n),
        in_specs=[HBM_SPEC] * (n + 1) + [pl.BlockSpec(memory_space=pl.ANY)],
        out_specs=[VMEM_SPEC] * (n + 1),
        out_shape=[pltpu.VMEM((PART, ROWS), jnp.float32)] * n + [MARK],
        scratch_shapes=[
            pltpu.VMEM((NSL, n * PART, SLW), jnp.bfloat16),
            pltpu.VMEM((NSL, ROWS, SLW), jnp.bfloat16),
            pltpu.VMEM((n * PART, ROWS), jnp.float32),
            pltpu.SemaphoreType.DMA((n, NSL)),
            pltpu.SemaphoreType.DMA((NSL,)),
        ],
        compiler_params=pltpu.CompilerParams(vmem_limit_bytes=20 << 20),
        cost_estimate=pl.CostEstimate(
            flops=2 * n * PART * ROWS * WIDTH, bytes_accessed=(10 << 20) + n * (3 << 19), transcendentals=0
        ),
        name="stream_products",
    )(*[in_hbm(part) for part in parts], in_hbm(rows), token)


def touch_kernel(rows_ref, token_ref, mark_ref):
    mark_ref[...] = jnp.zeros_like(mark_ref)


def touch(rows, token):
    return pl.pallas_call(
        touch_kernel,
        in_specs=[VMEM_SPEC, pl.BlockSpec(memory_space=pl.ANY)],
        out_specs=VMEM_SPEC,
        out_shape=MARK,
        compiler_params=pltpu.CompilerParams(vmem_limit_bytes=1 << 20),
        cost_estimate=pl.CostEstimate(flops=0, bytes_accessed=1 << 12, transcendentals=0),
        name="touch",
    )(in_vmem(rows), token)


def pack_kernel(first, batch, tab, *refs):
    *parts, _, out_ref, mark_ref, made, sem = refs
    mark_ref[...] = jnp.zeros_like(mark_ref)
    for n, (kind, _) in enumerate(batch):
        part = parts[n]
        for j in range(LOCAL):
            where = tab[T_PIECES + LOCAL * (first + n) + j]
            if kind == "V":
                made[where] = part[:, j * BLK : (j + 1) * BLK]
                continue
            for k in range(LOCAL):
                piece = part[j * PIECE : (j + 1) * PIECE, k * BLK : (k + 1) * BLK]
                made[where, k * PIECE : (k + 1) * PIECE, :] = piece
    copy = pltpu.make_async_copy(made, out_ref, sem)
    copy.start()
    copy.wait()


def pack(tab, first, batch, size, parts, token):
    return pl.pallas_call(
        functools.partial(pack_kernel, first, batch),
        in_specs=[SMEM_SPEC] + [VMEM_SPEC] * len(parts) + [pl.BlockSpec(memory_space=pl.ANY)],
        out_specs=[HBM_SPEC, VMEM_SPEC],
        out_shape=[pltpu.HBM((NCOL * size, PART, BLK), jnp.float32), MARK],
        scratch_shapes=[pltpu.VMEM((NCOL * size, PART, BLK), jnp.float32), pltpu.SemaphoreType.DMA],
        compiler_params=pltpu.CompilerParams(vmem_limit_bytes=6 << 20),
        cost_estimate=pl.CostEstimate(flops=0, bytes_accessed=3 << 20, transcendentals=0),
        name="pack",
    )(tab, *[in_vmem(part) for part in parts], token)


def place_tiles(tab, flags, number, sizes, ref, made, k):
    size = sizes[number]
    for n in range(size):
        at = T_SLOTS + 2 * (sum(sizes[:number]) + n)
        slot, kind = tab[at], tab[at + 1]
        weight = flags[SLOTS * k + slot].astype(jnp.float32)

        def tile(n=n, weight=weight):
            found = [ref[c * size + n, k * PIECE : (k + 1) * PIECE, :] for c in range(NCOL)]
            return jnp.concatenate(found, axis=0) * weight

        @pl.when(kind == 0)
        def _(slot=slot, tile=tile):
            made[k, pl.ds(slot, BLK, stride=SLOTS), :] = tile().T

        @pl.when(kind == 1)
        def _(slot=slot, tile=tile):
            made[k, pl.ds(slot, BLK, stride=SLOTS), :] = tile()


def early_kernel(sizes, tab, flags, *refs):
    count = len(refs) // 2 - 1
    given, made, pieces, sems = refs[:count], refs[count], refs[count + 1 : -1], refs[-1]
    copies = [pltpu.make_async_copy(ref, piece, sems.at[n]) for n, (ref, piece) in enumerate(zip(given, pieces))]
    for copy in copies:
        copy.start()
    for copy in copies:
        copy.wait()
    for k in range(LOCAL):
        for number, ref in enumerate(pieces):
            place_tiles(tab, flags, number, sizes, ref, made, k)


def place_early(tab, flags, sizes, pieces):
    return pl.pallas_call(
        functools.partial(early_kernel, sizes),
        in_specs=[SMEM_SPEC] * 2 + [HBM_SPEC] * len(pieces),
        out_specs=VMEM_SPEC,
        out_shape=pltpu.VMEM((LOCAL, BLK * SLOTS, BLK), jnp.float32),
        scratch_shapes=[pltpu.VMEM(piece.shape, jnp.float32) for piece in pieces]
        + [pltpu.SemaphoreType.DMA((len(pieces),))],
        compiler_params=pltpu.CompilerParams(vmem_limit_bytes=10 << 20),
        cost_estimate=pl.CostEstimate(flops=0, bytes_accessed=6 << 20, transcendentals=0),
        name="place_early",
    )(tab, flags, *[in_hbm(piece) for piece in pieces])


def late_kernel(sizes, tab, flags, early, piece, out_ref, made, sems, early_sem):
    def send(k):
        return pltpu.make_async_copy(made.at[k], out_ref.at[pl.ds(k * BLK * SLOTS, BLK * SLOTS), :], sems.at[k])

    copy = pltpu.make_async_copy(early, made, early_sem)
    copy.start()
    copy.wait()
    for k in range(LOCAL):
        place_tiles(tab, flags, len(sizes) - 1, sizes, piece, made, k)
        send(k).start()
    for k in range(LOCAL):
        send(k).wait()


def place_late(tab, flags, sizes, early, piece):
    return pl.pallas_call(
        functools.partial(late_kernel, sizes),
        in_specs=[SMEM_SPEC] * 2 + [VMEM_SPEC] * 2,
        out_specs=HBM_SPEC,
        out_shape=jax.ShapeDtypeStruct((ROWS * SLOTS, BLK), jnp.float32),
        scratch_shapes=[
            pltpu.VMEM((LOCAL, BLK * SLOTS, BLK), jnp.float32),
            pltpu.SemaphoreType.DMA((LOCAL,)),
            pltpu.SemaphoreType.DMA,
        ],
        compiler_params=pltpu.CompilerParams(vmem_limit_bytes=8 << 20),
        cost_estimate=pl.CostEstimate(flops=0, bytes_accessed=7 << 20, transcendentals=0),
        name="place_late",
    )(tab, flags, in_vmem(early), in_vmem(piece))


def flags_kernel(tab, pairs_ref, out_ref):
    first = jnp.minimum(pairs_ref[0:1, :], pairs_ref[1:2, :])
    second = jnp.maximum(pairs_ref[0:1, :], pairs_ref[1:2, :])
    codes = first * 256 + second
    for i in range(LOCAL):
        a = LOCAL * tab[0] + i
        for slot in range(SLOTS):
            b = tab[1] + NCOL * slot
            wanted = jnp.minimum(a, b) * 256 + jnp.maximum(a, b)
            out_ref[SLOTS * i + slot] = jnp.max((codes == wanted).astype(jnp.int32))


def listed_flags(tab, pair_list):
    return pl.pallas_call(
        flags_kernel,
        in_specs=[SMEM_SPEC, VMEM_SPEC],
        out_specs=SMEM_SPEC,
        out_shape=jax.ShapeDtypeStruct((LOCAL * SLOTS,), jnp.int32),
        compiler_params=pltpu.CompilerParams(vmem_limit_bytes=1 << 20),
        cost_estimate=pl.CostEstimate(flops=1 << 20, bytes_accessed=1 << 14, transcendentals=0),
        name="listed_flags",
    )(tab, pair_list.T)


def choose_kernel(tab, even_ref, odd_ref, out_ref, sem):
    core = lax.rem(tab[1], NCORE)
    for which, ref in enumerate((even_ref, odd_ref)):

        @pl.when(core == which)
        def _(ref=ref):
            pltpu.make_async_copy(ref, out_ref, sem).start()

    pltpu.make_async_copy(even_ref, out_ref, sem).wait()


def choose(tab, even, odd, late):
    return pl.pallas_call(
        choose_kernel,
        in_specs=[SMEM_SPEC] + [pl.BlockSpec(memory_space=pl.ANY)] * 2,
        out_specs=VMEM_SPEC,
        out_shape=pltpu.VMEM((PART, WIDTH), jnp.bfloat16),
        scratch_shapes=[pltpu.SemaphoreType.DMA],
        compiler_params=pltpu.CompilerParams(vmem_limit_bytes=4 << 20),
        cost_estimate=pl.CostEstimate(flops=0, bytes_accessed=5 << 19, transcendentals=0),
        name="choose",
    )(tab, in_hbm(even) if late else even, in_hbm(odd) if late else odd)


def per_device(coefficients, range_start, range_end, pair_list):
    sizes, table = tables()
    row, col = lax.axis_index("row"), lax.axis_index("col")
    tab = lax.dynamic_index_in_dim(jnp.asarray(table), row * NCOL + col, 0, keepdims=False)
    scalars = (in_hbm(tab), in_hbm(range_start), in_hbm(range_end))
    held = {0: own_part(*scalars[1:], coefficients)}
    rows, token = own_rows(scalars, coefficients)
    flags = listed_flags(tab, pair_list)
    made = {}

    def send(unit):
        a, b = UNITS[unit][2]
        source = held[a] if a == b else choose(tab, held[a], held[b], unit > 8)
        held[unit] = lax.ppermute(source, AXES, shifted(step_to(unit)))

    def multiply(group, token, how=products):
        *results, token = how([held[u] for u in group], rows, token)
        for unit, product in zip(group, results):
            made["U", unit] = product
        return token

    def send_back(unit):
        made["V", unit] = lax.ppermute(made["U", unit], AXES, shifted(step_back(unit)))

    def gate(units, token, back=()):
        found = [held[u] for u in units] + [made["V", u] for u in back]
        *values, token = lax.optimization_barrier((*found, token))
        held.update(zip(units, values))
        made.update({("V", u): value for u, value in zip(back, values[len(units) :])})
        return token

    for unit in (1, 2, 3, 4):
        send(unit)
    token = gate((1, 2, 3, 4), token)
    for unit in (5, 6, 7):
        send(unit)
    token = multiply(GROUPS[0], token)
    token = gate((5,), token)
    send(8)
    send(9)

    def ship(number, token):
        first = sum(len(earlier) for earlier in BATCHES[:number])
        batch = BATCHES[number]
        message, token = pack(tab, first, batch, sizes[number], [made[entry] for entry in batch], token)
        return lax.all_to_all(message, "col", 0, 0, tiled=True), token

    token = multiply(GROUPS[1], token)
    send_back(5)
    token = multiply(GROUPS[2], token)
    piece_a, token = ship(0, token)
    token = gate((8, 9), token)
    send(11)
    held[10] = tuple(lax.ppermute(held[u], AXES, shifted(step_to(10))[c::2]) for c, u in enumerate(UNITS[10][2]))
    token = multiply(GROUPS[3], token, stream_products)
    send_back(8)
    send_back(9)
    made["U", 7], token = lax.optimization_barrier((made["U", 7], token))
    send_back(7)
    token = touch(rows, token)
    token = multiply(GROUPS[4], token)
    piece_b, token = ship(1, token)
    early = place_early(tab, flags, sizes, [piece_a])
    return place_late(tab, flags, sizes, early, piece_b).reshape(ROWS, SLOTS, 1, BLK)


def solution(mesh):
    in_specs = (P("row", None, None), P(), P(), P())
    out_specs = P("row", None, "col", None)
    return jax.shard_map(per_device, mesh=mesh, in_specs=in_specs, out_specs=out_specs, check_vma=False)
```
